128 devices in a mesh: dp: 4 (over x), seq: 32 (over y, z, core).
Axes of the slice: x: 4, y: 4, z: 4, core: 2. Of those that a mesh axis runs over, the one named last changes fastest.
Arguments:
- query: bfloat16 [4, 8192, 1536], P('dp', 'seq'), may hold values from -9 to 9
- key: bfloat16 [4, 8192, 1536], P('dp', 'seq'), may hold values from -9 to 9
- value: bfloat16 [4, 8192, 1536], P('dp', 'seq'), may hold values from -16 to 16
- w_out: bfloat16 [1536, 1536], replicated, may hold values from -0.15625 to 0.15625
- grad_out: bfloat16 [4, 8192, 1536], P('dp', 'seq'), may hold values from -6 to 6
Outputs:
- mixed: bfloat16 [4, 8192, 1536], P('dp', 'seq')
- grad_query: bfloat16 [4, 8192, 1536], P('dp', 'seq')
- grad_key: bfloat16 [4, 8192, 1536], P('dp', 'seq')
- grad_value: bfloat16 [4, 8192, 1536], P('dp', 'seq')
- grad_weight: float32 [1536, 1536], P(('dp', 'seq'))
The draws below stay inside these ranges and needn't reach their ends.
All inputs are finite; a program needn't handle non-finite values.
Results may differ from the reference program's by a relative error of at most 0.025.
Values may be sent and summed in bfloat16 or wider, within the bound.
No kernel may reach another device: no remote copies, remote signals or barrier semaphores. Data moves between devices by JAX's collectives and lax.ppermute only.
A program may use at most 192 MiB of HBM per device.

```python
import math
import jax
import jax.numpy as jnp
from jax import lax

D = 1536
H = 12
HD = 128
BS = 32
TOK_DEV = 256
BATCH = 4
LENGTH = 8192


def draw_query(key, part):
    key = jax.random.fold_in(key, 11)
    rows = jnp.clip(jax.random.normal(key, (BATCH, LENGTH, D), jnp.float32), -6.0, 6.0)
    return rows.astype(jnp.bfloat16)


def draw_key(key, part):
    key = jax.random.fold_in(key, 12)
    rows = jnp.clip(jax.random.normal(key, (BATCH, LENGTH, D), jnp.float32), -6.0, 6.0)
    return rows.astype(jnp.bfloat16)


def draw_value(key, part):
    key = jax.random.fold_in(key, 13)
    regions = LENGTH // TOK_DEV
    region = jnp.clip(jax.random.normal(jax.random.fold_in(key, 1), (BATCH, regions, D), jnp.float32), -3.0, 3.0)
    region = jnp.repeat(region, TOK_DEV, axis=1)
    rows = jnp.clip(jax.random.normal(key, (BATCH, LENGTH, D), jnp.float32), -6.0, 6.0) + 2.0 * region
    return rows.astype(jnp.bfloat16)


def block_scale(key, extent, shards, least, high):
    def one(axis_at, shards_of):
        steps = jax.random.uniform(jax.random.fold_in(jax.random.fold_in(key, 6), axis_at), (shards_of,), jnp.float32, least / len(shards), high / len(shards))
        return jnp.repeat(jnp.exp(steps), extent[axis_at] // shards_of).reshape((-1,) + (1,) * (len(extent) - axis_at - 1))

    factor_of = one(*shards[0])
    for cut in shards[1:]:
        factor_of = factor_of * one(*cut)
    return factor_of


def bell_draw(stream_key, extent, scale, bound, cuts=(), held_as=jnp.bfloat16):
    entries = jax.random.normal(stream_key, extent, jnp.float32) * scale
    if len(cuts) > 0:
        entries = block_scale(stream_key, extent, cuts, -0.22, 0.18) * entries
    return jnp.clip(entries, min=-bound, max=bound).astype(held_as)


def setup_inputs(seed: int = 0) -> dict:
    streams_of = jax.random.split(jax.random.key(seed), 6)
    query = draw_query(jax.random.fold_in(streams_of[5], 71), 0)
    key = draw_key(jax.random.fold_in(streams_of[5], 71), 0)
    value = draw_value(jax.random.fold_in(streams_of[5], 71), 0)
    w_out = bell_draw(streams_of[3], (D, D), D ** -0.5, 0.15625)
    grad_out = bell_draw(streams_of[4], (BATCH, LENGTH, D), 1.0, 6.0, ((0, 4), (1, 32)))
    return {"query": query, "key": key, "value": value, "w_out": w_out, "grad_out": grad_out}


def pair_mean(rows):
    wide = rows.astype(jnp.float32).reshape(rows.shape[0] // 2, 2, rows.shape[1])
    return ((wide[:, 0] + wide[:, 1]) * 0.5).astype(jnp.bfloat16)

def spread_level(rows, level, blocks):
    width = rows.shape[1]
    nodes = rows.shape[0] // BS
    flipped = rows.reshape(nodes // 2, 2, BS, width)[:, ::-1].reshape(nodes, 1, BS, width)
    return jnp.broadcast_to(flipped, (nodes, 2 ** level, BS, width)).reshape(blocks, BS, width)

def collect_level(grads, level):
    blocks = grads.shape[0]
    width = grads.shape[2]
    nodes = blocks // 2 ** level
    summed = grads.reshape(nodes, 2 ** level, BS, width).sum(axis=1)
    return summed.reshape(nodes // 2, 2, BS, width)[:, ::-1].reshape(nodes * BS, width)

def fold_levels(grads, levels, length):
    width = grads.shape[2]
    carried = collect_level(grads[:, BS * levels:BS * (levels + 1)], levels - 1)
    for place in range(levels - 1, 0, -1):
        carried = jnp.repeat(carried, 2, axis=0) * 0.5 + collect_level(grads[:, BS * place:BS * (place + 1)], place - 1)
    return carried + grads[:, :BS].reshape(length, width)

def head_probs(head_queries, head_keys, score_bias):
    scale_factor = HD ** (-0.5)
    attention_logits = jnp.einsum('uzc,uhc->uzh', head_queries.astype(jnp.float32), head_keys.astype(jnp.float32)) * scale_factor + score_bias
    highest = lax.optimization_barrier(jnp.max(attention_logits, axis=-1, keepdims=True))
    expo = jnp.exp(attention_logits - highest)
    return expo / lax.optimization_barrier(jnp.sum(expo, axis=-1, keepdims=True))

def one_sequence(query, key, value, grad_out, w_out):
    length = query.shape[0]
    width = query.shape[1]
    blocks = length // BS
    levels = blocks.bit_length() - 1
    scale_factor = HD ** (-0.5)
    pairs = jnp.concatenate([key, value], axis=1)
    pyramid = [pairs]
    for level in range(levels - 1):
        pyramid.append(pair_mean(pyramid[-1]))
    key_set = jnp.concatenate([pairs.reshape(blocks, BS, 2 * width)] + [spread_level(pyramid[level], level, blocks) for level in range(levels)], axis=1)
    score_bias = jnp.concatenate([jnp.zeros((BS,), jnp.float32)] + [jnp.full((BS,), level * math.log(2.0), jnp.float32) for level in range(levels)])
    query_blocks = query.reshape(blocks, BS, width)

    def head_slices(head):
        head_queries = lax.dynamic_slice_in_dim(query_blocks, head * HD, HD, 2)
        head_keys = lax.dynamic_slice_in_dim(key_set, head * HD, HD, 2)
        head_values = lax.dynamic_slice_in_dim(key_set, width + head * HD, HD, 2)
        return (head_queries, head_keys, head_values)

    def forward_head(head):
        head_queries, head_keys, head_values = head_slices(head)
        probabilities = head_probs(head_queries, head_keys, score_bias)
        return jnp.einsum('mtf,mfn->mtn', probabilities.astype(jnp.bfloat16).astype(jnp.float32), head_values.astype(jnp.float32))
    heads = jnp.arange(H, dtype=jnp.int32)
    attended_f = lax.map(forward_head, heads)
    attended_f = jnp.transpose(attended_f, (1, 2, 0, 3)).reshape(length, width)
    attended = attended_f.astype(jnp.bfloat16)
    mixed = jnp.dot(attended, w_out, preferred_element_type=jnp.float32).astype(jnp.bfloat16)
    grad_attended = jnp.dot(grad_out, w_out.T, preferred_element_type=jnp.float32).astype(jnp.bfloat16)
    attended_blocks = attended_f.reshape(blocks, BS, width)
    grad_blocks = grad_attended.reshape(blocks, BS, width)

    def backward_head(head):
        head_queries, head_keys, head_values = head_slices(head)
        probabilities = head_probs(head_queries, head_keys, score_bias)
        probabilities_bfloat = probabilities.astype(jnp.bfloat16)
        head_gradient = lax.dynamic_slice_in_dim(grad_blocks, head * HD, HD, 2)
        attended_h = lax.dynamic_slice_in_dim(attended_blocks, head * HD, HD, 2)
        delta = lax.optimization_barrier(jnp.sum(head_gradient.astype(jnp.float32) * attended_h, axis=-1))
        probability_gradient = jnp.einsum('uzc,uhc->uzh', head_gradient.astype(jnp.float32), head_values.astype(jnp.float32))
        logit_gradient = (probabilities * (probability_gradient - delta[..., None]) * scale_factor).astype(jnp.bfloat16)
        query_head_gradient = jnp.einsum('mtf,mfn->mtn', logit_gradient.astype(jnp.float32), head_keys.astype(jnp.float32))
        key_set_gradient = jnp.einsum('rmf,rml->rfl', logit_gradient.astype(jnp.float32), head_queries.astype(jnp.float32))
        value_set_gradient = jnp.einsum('rmf,rml->rfl', probabilities_bfloat.astype(jnp.float32), head_gradient.astype(jnp.float32))
        return (query_head_gradient.reshape(length, HD), fold_levels(key_set_gradient, levels, length), fold_levels(value_set_gradient, levels, length))
    query_head_gradient, grad_key_h, grad_value_h = lax.map(backward_head, heads)
    grad_query = jnp.transpose(query_head_gradient, (1, 0, 2)).reshape(length, width).astype(jnp.bfloat16)
    grad_key = jnp.transpose(grad_key_h, (1, 0, 2)).reshape(length, width).astype(jnp.bfloat16)
    grad_value = jnp.transpose(grad_value_h, (1, 0, 2)).reshape(length, width).astype(jnp.bfloat16)
    weight_part = jnp.dot(attended.T, grad_out, preferred_element_type=jnp.float32)
    return (mixed, grad_query, grad_key, grad_value, weight_part)

def reference(query, key, value, w_out, grad_out):

    def per_sequence(items):
        return one_sequence(items[0], items[1], items[2], items[3], w_out)
    mixed, grad_query, grad_key, grad_value, weight_parts = lax.map(per_sequence, (query, key, value, grad_out))
    total = query.shape[0] * query.shape[1]
    grad_weight = lax.optimization_barrier(jnp.sum(weight_parts, axis=0)) * (1.0 / math.sqrt(total))
    return (mixed, grad_query, grad_key, grad_value, grad_weight)
```

```python
import math
import jax
import jax.numpy as jnp
from jax import lax
from jax.experimental import pallas as pl
from jax.experimental.pallas import tpu as pltpu
from jax.sharding import PartitionSpec as P
H=12; HD=128; BS=32; D=1536; T=256
BF=jnp.bfloat16; F=jnp.float32
HS=2
NT=(((1,),(1,)),((),()))
TN=(((0,),(0,)),((),()))
NN=(((1,),(0,)),((),()))
def mm(a,b,dims): return lax.dot_general(a,b,dims,preferred_element_type=F)

def head(q,k0,v0,k12,v12,xk,xv,ga,xbias,expand):
    scale=HD**-0.5
    kall=jnp.concatenate([k0,k12,xk],0)
    vall=jnp.concatenate([v0,v12,xv],0)
    s_all=mm(kall,q,NT)
    g_all=mm(vall,ga,NT)
    low=lax.broadcasted_iota(jnp.int32,(1,128),1)<64
    ln2=math.log(2.0)
    att=[];gq=[];ps=[];gs_=[];g0=[];g1=[];g2=[None,None]
    def pick(full,j):
        c=full[:,128*j:128*j+128]
        a=jnp.where(low,c[128*j:128*j+64],c[128*j+64:128*j+128])
        b=jnp.where(low,c[256+64*j+32:256+64*j+64],c[256+64*j:256+64*j+32])
        d=c[384+32*(1-j):384+32*(2-j)]
        return a,b,d,c[448:608]
    def widen(x):
        z=jnp.zeros_like(x[:64]); lowb=jnp.broadcast_to(low,(64,128)); lowc=jnp.broadcast_to(low,(32,128))
        a=x[:64]; b=x[64:96]; zb=jnp.zeros_like(b)
        return jnp.concatenate([jnp.where(lowb,a,z),jnp.where(lowb,z,a),jnp.where(lowc,zb,b),jnp.where(lowc,b,zb),x[96:]],0)
    for j in range(2):
        a,b,d,x=pick(s_all,j)
        s=jnp.concatenate([a*scale,b*scale+ln2,d*scale+2*ln2,x*scale+xbias],0)
        m=jnp.max(s,axis=0,keepdims=True)
        e=jnp.exp(s-m)
        l=jnp.sum(e,axis=0,keepdims=True)
        p=e*(1.0/l)
        pb=p.astype(BF)
        gp=jnp.concatenate(pick(g_all,j),0)
        delta=jnp.sum(pb.astype(F)*gp,axis=0,keepdims=True)
        gs=(p*(gp-delta)*scale).astype(BF)
        pw=widen(pb); gw=widen(gs)
        rows=slice(128*j,128*j+128); o=1-j
        kh=jnp.concatenate([k0[rows],k12[64*j:64*j+64],k12[128+32*o:160+32*o],xk],0)
        vh=jnp.concatenate([v0[rows],v12[64*j:64*j+64],v12[128+32*o:160+32*o],xv],0)
        att.append(mm(pw,vh,TN)); gq.append(mm(gw,kh,TN))
        gk=mm(gw[:224],q[rows],NN); gv=mm(pw[:224],ga[rows],NN)
        both=jnp.concatenate([gk,gv],1)
        g0.append(both[:128]); g1.append(both[128:192]); g2[o]=both[192:224]
        ps.append(pw[224:]); gs_.append(gw[224:])
    gxk=mm(jnp.concatenate(gs_,1),q,NN); gxv=mm(jnp.concatenate(ps,1),ga,NN)
    g0=jnp.concatenate(g0,0); g12=jnp.concatenate(g1+g2,0).astype(BF)
    fine=g0+mm(expand,g12,NN)
    return jnp.concatenate(att,0),jnp.concatenate(gq,0),fine[:,:128],fine[:,128:],gxk,gxv

def expansion():
    r=lax.broadcasted_iota(jnp.int32,(T,192),0); c=lax.broadcasted_iota(jnp.int32,(T,192),1)
    return jnp.where(c<128,jnp.where((r>>1)==c,0.5,0.0),jnp.where((r>>2)==c-128,0.25,0.0)).astype(BF)

def attention_kernel(q,k0,v0,k12,v12,xk,xv,ga,go,att_o,gq_o,fk_o,fv_o,gxk_o,gxv_o,gw_o):
    expand=expansion()
    r=lax.broadcasted_iota(jnp.int32,(160,1),0)
    ln2=math.log(2.0)
    xb=(3+ (r>>5)).astype(F)*ln2
    for i in range(HS):
        c=slice(i*HD,i*HD+HD)
        att,gq,fk,fv,gxk,gxv=head(q[:,c],k0[:,c],v0[:,c],k12[:,c],v12[:,c],xk[:,c],xv[:,c],ga[:,c],xb,expand)
        attb=att.astype(BF)
        att_o[:,c]=attb; gq_o[:,c]=gq.astype(BF); fk_o[:,c]=fk; fv_o[:,c]=fv
        gxk_o[:,c]=gxk; gxv_o[:,c]=gxv
        gw_o[i*HD:i*HD+HD,:]=mm(attb,go[...],TN).astype(BF)

def attention(q,k,v,l12,xs,ga,go):
    W=HS*HD; n=H//HS
    def sp(rows,off=0): return pl.BlockSpec((rows,W),lambda h:(0,h+off))
    return pl.pallas_call(attention_kernel,grid=(n,),
        in_specs=[sp(T),sp(T),sp(T),sp(192),sp(192,n),sp(160),sp(160,n),sp(T),pl.BlockSpec((T,D),lambda h:(0,0))],
        out_specs=[sp(T),sp(T),sp(T),sp(T),sp(160),sp(160),pl.BlockSpec((W,D),lambda h:(h,0))],
        out_shape=[jax.ShapeDtypeStruct((T,D),BF)]*2+[jax.ShapeDtypeStruct((T,D),F)]*2+[jax.ShapeDtypeStruct((160,D),F)]*2+[jax.ShapeDtypeStruct((D,D),BF)],
        compiler_params=pltpu.CompilerParams(vmem_limit_bytes=48*2**20),name="attention")(q,k,v,l12,l12,xs,xs,ga,go)

def pyramid_kernel(k,v,l12,l3):
    def avg(n):
        r=lax.broadcasted_iota(jnp.int32,(n,2*n),0); c=lax.broadcasted_iota(jnp.int32,(n,2*n),1)
        return jnp.where((c>>1)==r,0.5,0.0).astype(BF)
    a1,a2,a3=avg(128),avg(64),avg(32)
    for i,x in enumerate((k,v)):
        c=slice(i*D,i*D+D)
        x1=mm(a1,x[...],NN).astype(BF); x2=mm(a2,x1,NN).astype(BF); x3=mm(a3,x2,NN).astype(BF)
        l12[:128,c]=x1; l12[128:,c]=x2; l3[:,c]=x3

def pyramid(k,v):
    return pl.pallas_call(pyramid_kernel,out_shape=[jax.ShapeDtypeStruct((192,2*D),BF),jax.ShapeDtypeStruct((32,2*D),BF)],
        compiler_params=pltpu.CompilerParams(vmem_limit_bytes=48*2**20),name="pyramid")(k,v)


def fold_matrix(n):
    r = lax.broadcasted_iota(jnp.int32, (n, 2 * n), 0)
    c = lax.broadcasted_iota(jnp.int32, (n, 2 * n), 1)
    return jnp.where((c >> 1) == r, 0.5, 0.0).astype(BF)


def spread_matrix(n, bits):
    r = lax.broadcasted_iota(jnp.int32, (n << bits, n), 0)
    c = lax.broadcasted_iota(jnp.int32, (n << bits, n), 1)
    return jnp.where((r >> bits) == c, 0.5**bits, 0.0).astype(BF)


def chip_kernel(mine, other, l4, l5):
    x = jnp.concatenate([mine[...], other[...]], 0)
    x = mm(fold_matrix(32), x, NN).astype(BF)
    l4[...] = x
    l5[...] = mm(fold_matrix(16), x, NN).astype(BF)


def row_kernel(l5, z1, z2, z3, l6, l7):
    x = jnp.concatenate([l5[...], mm(fold_matrix(16), z1[...], NN).astype(BF), z2[...], z3[...]], 0)
    x = mm(fold_matrix(32), x, NN).astype(BF)
    l6[...] = x
    l7[...] = mm(fold_matrix(16), x, NN).astype(BF)


def spread(x, bits):
    return mm(spread_matrix(x.shape[0], bits), x.astype(BF), NN)


def back_row_kernel(gk, gv, y1, y2, y3, s1, s2, s3, own):
    g6 = y1[...].astype(F) + spread(y2[...].astype(F) + y3[...].astype(F), 1)
    for i, g in enumerate((gk, gv)):
        c = slice(i * D, i * D + D)
        s1[:, c] = (g[32:64, :] + spread(g6[8:16, c], 2)).astype(BF)
        s2[:, c] = (g[64:80, :] + spread(g6[16:24, c], 1)).astype(BF)
        s3[:, c] = (g[80:96, :] + spread(g6[24:32, c], 1)).astype(BF)
        own[:, c] = spread(g6[:8, c], 2)


def back_chip_kernel(gk, gv, own, z1, z2, z3, send, keep):
    g4 = own[...] + z1[...].astype(F) + spread(z2[...].astype(F) + z3[...].astype(F), 1)
    for i, g in enumerate((gk, gv)):
        c = slice(i * D, i * D + D)
        send[:, c] = (g[:32, :] + spread(g4[16:, c], 1)).astype(BF)
        keep[:, c] = spread(g4[:16, c], 1)


def finish_kernel(fk, fv, keep, c1, ok, ov):
    g3 = keep[...] + c1[...].astype(F)
    for i, (f, o) in enumerate(((fk, ok), (fv, ov))):
        c = slice(i * D, i * D + D)
        o[...] = (f[...] + spread(g3[:, c], 3)).astype(BF)


def small(kernel, shapes, name):
    return pl.pallas_call(
        kernel,
        out_shape=[jax.ShapeDtypeStruct(s, t) for s, t in shapes],
        compiler_params=pltpu.CompilerParams(vmem_limit_bytes=48 * 2**20),
        name=name,
    )


def across(x, flip):
    return lax.ppermute(x, "seq", [(i, i ^ flip) for i in range(32)])


def along_x(x, step):
    return lax.ppermute(x, "dp", [(i, (i + step) % 4) for i in range(4)])


def along_y(x, step):
    return lax.ppermute(x, "seq", [(i, (i + 8 * step) % 32) for i in range(32)])


def along_z(x, step):
    return lax.ppermute(x, "seq", [(i, i // 8 * 8 + (i + 2 * step) % 8) for i in range(32)])


def scatter_four(rows, move, place):
    n = rows.shape[0] // 4

    def part(i):
        return lax.dynamic_slice_in_dim(rows, i % 4 * n, n, 0)

    total = part(place).astype(F)
    for step in (1, 2, 3):
        total = total + move(part(place + step), step).astype(F)
    return total


def local(query, key, value, w_out, grad_out):
    q, k, v, go = query[0], key[0], value[0], grad_out[0]
    place = lax.axis_index("seq")
    l12, l3 = pyramid(k, v)
    c1 = across(l3, 1)
    ga = mm(go, w_out, NT).astype(BF)
    W = 2 * D
    l4, l5 = small(chip_kernel, [((32, W), BF), ((16, W), BF)], "chip")(l3, c1)
    z1, z2, z3 = across(l4, 2), across(l5, 4), across(l5, 6)
    l6, l7 = small(row_kernel, [((32, W), BF), ((16, W), BF)], "row")(l5, z1, z2, z3)
    y1, y2, y3 = across(l6, 8), across(l7, 16), across(l7, 24)
    xs = jnp.concatenate([c1, z1, z2, z3, y1, y2, y3], 0)
    att, gq, fk, fv, gxk, gxv, gw = attention(q, k, v, l12, xs, ga, go)
    gxb = jnp.concatenate([gxk[96:], gxv[96:]], 1).astype(BF)
    y1, y2, y3 = across(gxb[:32], 8), across(gxb[32:48], 16), across(gxb[48:], 24)
    s1, s2, s3, own = small(
        back_row_kernel, [((32, W), BF), ((16, W), BF), ((16, W), BF), ((32, W), F)], "back_row"
    )(gxk, gxv, y1, y2, y3)
    z1, z2, z3 = across(s1, 2), across(s2, 4), across(s3, 6)
    send, keep = small(back_chip_kernel, [((32, W), BF), ((32, W), F)], "back_chip")(
        gxk, gxv, own, z1, z2, z3
    )
    c1 = across(send, 1)
    gk, gv = small(finish_kernel, [((T, D), BF), ((T, D), BF)], "finish")(fk, fv, keep, c1)
    mixed = mm(att, w_out, NN).astype(BF)
    core = place % 2
    half = D // 2
    mine = lax.dynamic_slice_in_dim(gw, core * half, half, 1)
    theirs = lax.dynamic_slice_in_dim(gw, (1 - core) * half, half, 1)
    part = (mine.astype(F) + across(theirs, 1).astype(F)).astype(BF)
    part = scatter_four(part, along_x, lax.axis_index("dp")).astype(BF)
    part = scatter_four(part, along_y, place // 8).astype(BF)
    part = scatter_four(part, along_z, place // 2 % 4)
    first = core == 0
    mine = jnp.where(first, part[:12], part[12:])
    theirs = across(jnp.where(first, part[12:], part[:12]), 1)
    total = jnp.concatenate([jnp.where(first, mine, theirs), jnp.where(first, theirs, mine)], 1)
    gw = total * (1.0 / math.sqrt(4 * 32 * T))
    return mixed[None], gq[None], gk[None], gv[None], gw


def solution(mesh):
    rows = P("dp", "seq", None)
    return jax.shard_map(
        local,
        mesh=mesh,
        in_specs=(rows, rows, rows, P(), rows),
        out_specs=(rows, rows, rows, rows, P(("dp", "seq"), None)),
        check_vma=False,
    )
```

```python
import math

import jax
import jax.numpy as jnp
from jax import lax
from jax.experimental import pallas as pl
from jax.experimental.pallas import tpu as pltpu
from jax.sharding import PartitionSpec as P

H = 12
HD = 128
D = 1536
T = 256
HS = 2
W = HS * HD
STEPS = H // HS
BF = jnp.bfloat16
F = jnp.float32
NT = (((1,), (1,)), ((), ()))
TN = (((0,), (0,)), ((), ()))
NN = (((1,), (0,)), ((), ()))
LN2 = math.log(2.0)
SCALE = HD**-0.5
PART = D // 4
PAIR = 2 * D


def mm(a, b, dims):
    return lax.dot_general(a, b, dims, preferred_element_type=F)


def params(mib):
    return pltpu.CompilerParams(vmem_limit_bytes=mib * 2**20)


def cost(us):
    return pl.CostEstimate(flops=0, bytes_accessed=int(us * 3.7e6), transcendentals=0)


def shapes(*items):
    return [jax.ShapeDtypeStruct(s, t) for s, t in items]


def fold_matrix(n):
    r = lax.broadcasted_iota(jnp.int32, (n, 2 * n), 0)
    c = lax.broadcasted_iota(jnp.int32, (n, 2 * n), 1)
    return jnp.where((c >> 1) == r, 0.5, 0.0).astype(BF)


def fold(x):
    return mm(fold_matrix(x.shape[0] // 2), x, NN).astype(BF)


def spread(x, bits):
    n = x.shape[0]
    r = lax.broadcasted_iota(jnp.int32, (n << bits, n), 0)
    c = lax.broadcasted_iota(jnp.int32, (n << bits, n), 1)
    return mm(jnp.where((r >> bits) == c, 0.5**bits, 0.0).astype(BF), x.astype(BF), NN)


def pyramid_kernel(k, v, l12, l3, rows, sems):
    copies = []
    for step in range(STEPS):
        for i, x in enumerate((k, v)):
            n = 2 * step + i
            copies.append(
                pltpu.make_async_copy(x.at[:, pl.ds(step * W, W)], rows.at[:, pl.ds(n * W, W)], sems.at[n])
            )
            copies[-1].start()
    for part in range(3):
        c = slice(part * 4 * W, part * 4 * W + 4 * W)
        for copy in copies[4 * part : 4 * part + 4]:
            copy.wait()
        x1 = fold(rows[:, c])
        x2 = fold(x1)
        l12[:128, c] = x1
        l12[128:, c] = x2
        l3[:, c] = fold(x2)


def pyramid(k, v):
    far = pl.BlockSpec(memory_space=pl.ANY)
    near = pl.BlockSpec(memory_space=pltpu.VMEM)
    return pl.pallas_call(
        pyramid_kernel,
        in_specs=[far, far],
        out_specs=[near, near],
        out_shape=shapes(((192, PAIR), BF), ((32, PAIR), BF)),
        scratch_shapes=[pltpu.VMEM((T, PAIR), BF), pltpu.SemaphoreType.DMA((2 * STEPS,))],
        cost_estimate=cost(1.9),
        compiler_params=params(10),
        name="pyramid",
    )(k, v)


def chip_kernel(mine, other, l4, l5):
    x = fold(jnp.concatenate([mine[...], other[...]], 0))
    l4[...] = x
    l5[...] = fold(x)


def row_kernel(l5, z1, z2, z3, l6, l7):
    x = fold(jnp.concatenate([l5[...], fold(z1[...]), z2[...], z3[...]], 0))
    l6[...] = x
    l7[...] = fold(x)


def head(q, k0, v0, k12, v12, xk, xv, ga, bias, expand):
    s_all = mm(jnp.concatenate([k0, k12, xk], 0), q, NT)
    g_all = mm(jnp.concatenate([v0, v12, xv], 0), ga, NT)
    low = lax.broadcasted_iota(jnp.int32, (1, 128), 1) < 64
    low64 = jnp.broadcast_to(low, (64, 128))
    low32 = low64[:32]

    def pick(full, j):
        c = full[:, 128 * j : 128 * j + 128]
        a = jnp.where(low, c[128 * j : 128 * j + 64], c[128 * j + 64 : 128 * j + 128])
        b = jnp.where(low, c[288 + 64 * j : 320 + 64 * j], c[256 + 64 * j : 288 + 64 * j])
        d = c[416 - 32 * j : 448 - 32 * j]
        return jnp.concatenate([a, b, d, c[448:608]], 0)

    def widen(x):
        a, b = x[:64], x[64:96]
        za, zb = jnp.zeros_like(a), jnp.zeros_like(b)
        return jnp.concatenate(
            [
                jnp.where(low64, a, za),
                jnp.where(low64, za, a),
                jnp.where(low32, zb, b),
                jnp.where(low32, b, zb),
                x[96:],
            ],
            0,
        )

    att, gq, g0, g1, g2, px, sx = [], [], [], [], [None, None], [], []
    for j in range(2):
        s = pick(s_all, j) * SCALE + bias
        e = jnp.exp(s - jnp.max(s, axis=0, keepdims=True))
        p = e * (1.0 / jnp.sum(e, axis=0, keepdims=True))
        pb = p.astype(BF)
        gp = pick(g_all, j)
        delta = jnp.sum(pb.astype(F) * gp, axis=0, keepdims=True)
        gs = (p * (gp - delta) * SCALE).astype(BF)
        pw, sw = widen(pb), widen(gs)
        rows, o = slice(128 * j, 128 * j + 128), 1 - j
        near = slice(64 * j, 64 * j + 64)
        far = slice(128 + 32 * o, 160 + 32 * o)
        kh = jnp.concatenate([k0[rows], k12[near], k12[far], xk], 0)
        vh = jnp.concatenate([v0[rows], v12[near], v12[far], xv], 0)
        att.append(mm(pw, vh, TN))
        gq.append(mm(sw, kh, TN))
        both = jnp.concatenate([mm(sw[:224], q[rows], NN), mm(pw[:224], ga[rows], NN)], 1)
        g0.append(both[:128])
        g1.append(both[128:192])
        g2[o] = both[192:224]
        px.append(pw[224:])
        sx.append(sw[224:])
    gxk = mm(jnp.concatenate(sx, 1), q, NN)
    gxv = mm(jnp.concatenate(px, 1), ga, NN)
    coarse = jnp.concatenate(g1 + g2, 0).astype(BF)
    fine = jnp.concatenate(g0, 0) + mm(expand, coarse, NN)
    return jnp.concatenate(att, 0), jnp.concatenate(gq, 0), fine, gxk, gxv


def attention_kernel(base, q, k, v, l12, c1, z1, z2, z3, y1, y2, y3, ga, *rest):
    att_o, gq_o, fine_o, gc_o, gz_o, gy1_o, gy2_o, gy3_o, attt_o = rest[-9:]
    r = lax.broadcasted_iota(jnp.int32, (T, 192), 0)
    c = lax.broadcasted_iota(jnp.int32, (T, 192), 1)
    half = jnp.where((r >> 1) == c, 0.5, 0.0)
    expand = jnp.where(c < 128, half, jnp.where((r >> 2) == c - 128, 0.25, 0.0)).astype(BF)
    r = lax.broadcasted_iota(jnp.int32, (288, 1), 0)
    bias = jnp.where(r < 64, 0, (r >> 5) - 1).astype(F) * LN2
    x = jnp.concatenate([c1[...], z1[...], z2[...], z3[...], y1[...], y2[...], y3[...]], 0)
    for i in range(HS):
        c = slice(i * HD, i * HD + HD)
        cv = slice(W + i * HD, W + i * HD + HD)
        att, gq, fine, gxk, gxv = head(
            q[:, c], k[:, c], v[:, c], l12[:, c], l12[:, cv], x[:, c], x[:, cv], ga[:, c], bias, expand
        )
        att_o[:, c] = att.astype(BF)
        attt_o[c, :] = jnp.transpose(att).astype(BF)
        gq_o[:, c] = gq.astype(BF)
        for cols, g, f in ((c, gxk, fine[:, :HD]), (cv, gxv, fine[:, HD:])):
            fine_o[:, cols] = f
            gc_o[:, cols] = g[:32]
            gz_o[:, cols] = g[32:96]
            gy1_o[:, cols] = g[96:128].astype(BF)
            gy2_o[:, cols] = g[128:144].astype(BF)
            gy3_o[:, cols] = g[144:].astype(BF)


def attention(bits, flip, q, k, v, l12, pieces, ga, begun=()):
    def cols(rows, wide=W):
        return pl.BlockSpec((rows, wide), lambda h, s: (0, h + (s[XH] ^ flip) * (STEPS // 2)))

    outs = shapes(
        ((T, D), BF),
        ((T, D), BF),
        ((T, PAIR), F),
        ((32, PAIR), F),
        ((64, PAIR), F),
        ((32, PAIR), BF),
        ((16, PAIR), BF),
        ((16, PAIR), BF),
        ((D // 2, T), BF),
    )
    operands = (q, k, v, l12, *pieces, ga)
    return pl.pallas_call(
        attention_kernel,
        grid_spec=pltpu.PrefetchScalarGridSpec(
            num_scalar_prefetch=1,
            grid=(STEPS // 2,),
            in_specs=[cols(T)] * 3
            + [cols(192, 2 * W)]
            + [cols(p.shape[0], 2 * W) for p in pieces]
            + [cols(T)]
            + [pl.BlockSpec(memory_space=pl.ANY)] * len(begun),
            out_specs=[cols(T), cols(T)]
            + [cols(n, 2 * W) for n in (T, 32, 64, 32, 16, 16)]
            + [pl.BlockSpec((W, T), lambda h, s: (h, 0))],
        ),
        out_shape=outs,
        input_output_aliases={1 + len(operands) + i: i for i in range(len(begun))},
        cost_estimate=cost(7),
        compiler_params=params(24),
        name="attention",
    )(bits, *operands, *begun)


def back_row_kernel(gz, y1, y2, y3, s1, s2, s3, own):
    g6 = y1[...].astype(F) + spread(y2[...].astype(F) + y3[...].astype(F), 1)
    s1[...] = (gz[:32, :] + spread(g6[8:16], 2)).astype(BF)
    s2[...] = (gz[32:48, :] + spread(g6[16:24], 1)).astype(BF)
    s3[...] = (gz[48:, :] + spread(g6[24:], 1)).astype(BF)
    own[...] = spread(g6[:8], 2)


def back_chip_kernel(gc, own, z1, z2, z3, send, keep):
    g4 = own[...] + z1[...].astype(F) + spread(z2[...].astype(F) + z3[...].astype(F), 1)
    send[...] = (gc[...] + spread(g4[16:], 1)).astype(BF)
    keep[...] = spread(g4[:16], 1)


def finish_kernel(fine, keep, c1, gk, gv):
    g3 = keep[...] + c1[...].astype(F)
    for step in range(STEPS):
        for i, out in enumerate((gk, gv)):
            c = slice((2 * step + i) * W, (2 * step + i) * W + W)
            out[:, step * W : step * W + W] = (fine[:, c] + spread(g3[:, c], 3)).astype(BF)


def split_kernel(bits, go, go_m, go_o):
    mine = bits[CORE]
    half = D // 2
    go_m[...] = go[:, pl.ds(pl.multiple_of(mine * half, half), half)]
    go_o[...] = go[:, pl.ds(pl.multiple_of((1 - mine) * half, half), half)]


def split(bits, go):
    vmem = pl.BlockSpec(memory_space=pltpu.VMEM)
    return pl.pallas_call(
        split_kernel,
        in_specs=[pl.BlockSpec(memory_space=pltpu.SMEM), vmem],
        out_specs=[vmem] * 2,
        out_shape=shapes(*[((T, D // 2), BF)] * 2),
        cost_estimate=cost(0.3),
        compiler_params=params(10),
        name="split",
    )(bits, go)


def grad_attended_kernel(go, w, ga):
    for c in range(0, D, 256):
        ga[:, c : c + 256] = mm(go[...], w[c : c + 256, :], NT).astype(BF)


def mixed_kernel(att, w, out):
    for c in range(0, D, 256):
        out[:, c : c + 256] = mm(att[...], w[:, c : c + 256], NN).astype(BF)


def small(kernel, outs, name, us=0.4):
    return pl.pallas_call(kernel, out_shape=shapes(*outs), cost_estimate=cost(us),
        compiler_params=params(12), name=name)


def halves(which, outer, half):
    for o in range(outer):
        first = pl.multiple_of((2 * o + which) * half, 16 if half % 16 == 0 else 8)
        yield slice(o * half, o * half + half), pl.ds(first, half)


def weight_kernel(bits, *refs, color, bit, outer, half):
    send, keep = refs[-2:]
    n = (len(refs) - 2) // 2
    atts, gos = refs[:n], refs[n : 2 * n]
    away = 1 - bits[bit]
    c = slice(color * PART, color * PART + PART)
    for out, which in ((send, away), (keep, 1 - away)):
        for to, rows in halves(which, outer, half):
            out[to, :] = sum(mm(a[rows, :], g[:, c], NN) for a, g in zip(atts, gos, strict=True)).astype(BF)


def weight(bits, atts, gos, color, bit, outer, half):
    vmem = pl.BlockSpec(memory_space=pltpu.VMEM)
    return pl.pallas_call(
        lambda *refs: weight_kernel(*refs, color=color, bit=bit, outer=outer, half=half),
        in_specs=[pl.BlockSpec(memory_space=pltpu.SMEM)] + [vmem] * (2 * len(atts)),
        out_specs=[vmem, vmem],
        out_shape=shapes(((D // 4, PART), BF), ((D // 4, PART), BF)),
        cost_estimate=cost(1.5),
        compiler_params=params(10),
        name="weight_part",
    )(bits, *atts, *gos)


def merge_kernel(bits, *refs, bit, outer, half):
    away = 1 - bits[bit]
    n = (len(refs) - 2) // 2
    for out, which in ((refs[-2], away), (refs[-1], 1 - away)):
        for to, rows in halves(which, outer, half):
            for i in range(n):
                a, b = refs[2 * i], refs[2 * i + 1]
                w = a.shape[1]
                s = a[rows, :].astype(F) + b[rows, :].astype(F)
                out[to, i * w : i * w + w] = s.astype(out.dtype)


def merge(bits, pairs, bit, outer, half, dtype=BF):
    operands = [x for pair in pairs for x in pair]
    wide = sum(pair[0].shape[1] for pair in pairs)
    vmem = pl.BlockSpec(memory_space=pltpu.VMEM)
    return pl.pallas_call(
        lambda *refs: merge_kernel(*refs, bit=bit, outer=outer, half=half),
        in_specs=[pl.BlockSpec(memory_space=pltpu.SMEM)] + [vmem] * len(operands),
        out_specs=[vmem, vmem],
        out_shape=shapes(*[((outer * half, wide), dtype)] * 2),
        cost_estimate=cost(0.6),
        compiler_params=params(10),
        name="merge",
    )(bits, *operands)


def last_merge_kernel(bits, a_k, a_r, b_k, b_r, *outs):
    y, z = bits[YL], bits[ZL]
    total = jnp.concatenate(
        [a_k[...].astype(F) + a_r[...].astype(F), b_k[...].astype(F) + b_r[...].astype(F)], 1
    )
    quarters = [total[24 * i : 24 * i + 24] for i in range(4)]
    for out, dy, dz in zip(outs, (1, 0, 1, 0), (0, 1, 1, 0), strict=True):
        low = [jnp.where((z ^ dz) == 0, quarters[2 * i], quarters[2 * i + 1]) for i in range(2)]
        out[...] = jnp.where((y ^ dy) == 0, low[0], low[1])


def last_merge(bits, *operands):
    vmem = pl.BlockSpec(memory_space=pltpu.VMEM)
    return pl.pallas_call(
        last_merge_kernel,
        in_specs=[pl.BlockSpec(memory_space=pltpu.SMEM)] + [vmem] * 4,
        out_specs=[vmem] * 4,
        out_shape=shapes(*[((24, D // 2), F)] * 4),
        cost_estimate=cost(0.6),
        compiler_params=params(10),
        name="last_merge",
    )(bits, *operands)


def after(x, *others):
    return lax.optimization_barrier((x, *others))[0]


def across(x, flip):
    return lax.ppermute(x, "seq", [(i, i ^ flip) for i in range(32)])


def across_x(x, flip):
    return lax.ppermute(x, "dp", [(i, i ^ flip) for i in range(4)])


XH, XL, YH, YL, ZH, ZL, CORE = range(7)


def local(query, key, value, w_out, grad_out):
    q, k, v, go = query[0], key[0], value[0], grad_out[0]
    place = lax.axis_index("seq")
    row = lax.axis_index("dp")
    core = place & 1
    bits = jnp.stack(
        [row >> 1, row & 1, place >> 4 & 1, place >> 3 & 1, place >> 2 & 1, place >> 1 & 1, core]
    ).astype(jnp.int32)
    l12, l3 = pyramid(after(k, bits), v)
    c1 = across(l3, 1)
    l4, l5 = small(chip_kernel, [((32, PAIR), BF), ((16, PAIR), BF)], "chip")(l3, c1)
    z1, z3, z2 = across(l4, 2), across(l5, 6), across(l5, 4)
    go_m, go_s = split(bits, after(go, l3))
    go_o = across(go_s, 1)
    l5 = after(l5, go_o)
    ga = small(grad_attended_kernel, [((T, D), BF)], "grad_attended", 2.0)(after(go, z1), w_out)[0]
    l6, l7 = small(row_kernel, [((32, PAIR), BF), ((16, PAIR), BF)], "row")(l5, z1, z2, z3)
    gox_m, gox_o = across_x(go_m, 3), across_x(go_o, 3)
    y1, y3, y2 = across(l6, 8), across(l7, 24), across(l7, 16)
    pieces = (c1, z1, z2, z3, y1, y2, y3)
    *begun, sent = attention(bits, 1, after(q, gox_m), k, v, l12, pieces, ga)
    att_x = across_x(sent, 3)
    att, gq, fine, gc, gz, gy1, gy2, gy3, att_m = attention(
        bits, 0, after(q, gox_o), k, v, l12, pieces, ga, begun
    )
    att_o, att_xo = across(att_m, 1), across(att_x, 1)
    y1, y3, y2 = across(gy1, 8), across(gy3, 24), across(gy2, 16)
    atts = (att_m, att_o, att_x, att_xo)
    gos = (go_m, go_o, gox_m, gox_o)
    b_s, b_k = weight(bits, atts, gos, 1, ZH, 8, 48)
    b_r = across(b_s, 6)
    a_s, a_k = weight(bits, (after(att_m, b_k), *atts[1:]), gos, 0, XL, 1, 384)
    a_r = across_x(a_s, 1)
    s1, s2, s3, own = small(
        back_row_kernel, [((32, PAIR), BF), ((16, PAIR), BF), ((16, PAIR), BF), ((32, PAIR), F)], "back_row"
    )(after(gz, a_k), y1, y2, y3)
    z1, z3, z2 = across(s1, 2), across(s3, 6), across(s2, 4)
    b_s, b_k = merge(bits, [(after(b_k, own), b_r)], YH, 2, 96)
    b_r = across(b_s, 24)
    a_s, a_k = merge(bits, [(after(a_k, b_k), a_r)], ZH, 4, 48)
    a_r = across(a_s, 6)
    mixed = small(mixed_kernel, [((T, D), BF)], "mixed", 2.3)(after(att, a_k), w_out)[0]
    send, keep = small(back_chip_kernel, [((32, PAIR), BF), ((32, PAIR), F)], "back_chip")(
        after(gc, mixed), own, z1, z2, z3
    )
    c1 = across(send, 1)
    b_s, b_k = merge(bits, [(after(b_k, keep), b_r)], XL, 1, 96)
    b_r = across_x(b_s, 1)
    a_s, a_k = merge(bits, [(after(a_k, b_k), a_r)], YH, 1, 96)
    a_r = across(a_s, 24)
    gk, gv = small(finish_kernel, [((T, D), BF), ((T, D), BF)], "finish", 1.7)(after(fine, a_k), keep, c1)
    s1, s2, s3, kept = last_merge(bits, after(a_k, gk), a_r, b_k, b_r)
    part = kept + across(s1, 8) + across(s2, 2) + across(s3, 10)
    first = core == 0
    mine = jnp.where(first, part[:12], part[12:])
    theirs = across(jnp.where(first, part[12:], part[:12]), 1)
    total = jnp.concatenate([jnp.where(first, mine, theirs), jnp.where(first, theirs, mine)], 1)
    gw = total * (1.0 / math.sqrt(4 * 32 * T))
    return mixed[None], gq[None], gk[None], gv[None], gw


def solution(mesh):
    rows = P("dp", "seq", None)
    return jax.shard_map(
        local,
        mesh=mesh,
        in_specs=(rows, rows, rows, P(), rows),
        out_specs=(rows, rows, rows, rows, P(("dp", "seq"), None)),
        check_vma=False,
    )
```

```python
import math

import jax
import jax.numpy as jnp
from jax import lax
from jax.experimental import pallas as pl
from jax.experimental.pallas import tpu as pltpu
from jax.sharding import PartitionSpec as P

H = 12
HD = 128
D = 1536
T = 256
HS = 2
W = HS * HD
STEPS = H // HS
HALF_STEPS = STEPS // 2
UNROLL = True
BF = jnp.bfloat16
F = jnp.float32
NT = (((1,), (1,)), ((), ()))
TN = (((0,), (0,)), ((), ()))
NN = (((1,), (0,)), ((), ()))
LN2 = math.log(2.0)
SCALE = HD**-0.5
PART = D // 4
PAIR = 2 * D


def mm(a, b, dims):
    return lax.dot_general(a, b, dims, preferred_element_type=F)


def params(mib):
    return pltpu.CompilerParams(vmem_limit_bytes=mib * 2**20)


def cost(us):
    return pl.CostEstimate(flops=0, bytes_accessed=int(us * 3.7e6), transcendentals=0)


def shapes(*items):
    return [jax.ShapeDtypeStruct(s, t) for s, t in items]


def fold_matrix(n):
    r = lax.broadcasted_iota(jnp.int32, (n, 2 * n), 0)
    c = lax.broadcasted_iota(jnp.int32, (n, 2 * n), 1)
    return jnp.where((c >> 1) == r, 0.5, 0.0).astype(BF)


def fold(x):
    return mm(fold_matrix(x.shape[0] // 2), x, NN).astype(BF)


def spread(x, bits):
    n = x.shape[0]
    r = lax.broadcasted_iota(jnp.int32, (n << bits, n), 0)
    c = lax.broadcasted_iota(jnp.int32, (n << bits, n), 1)
    return mm(jnp.where((r >> bits) == c, 0.5**bits, 0.0).astype(BF), x.astype(BF), NN)


def pyramid_kernel(k, v, l12, l3, rows, sems):
    copies = []
    for step in range(STEPS):
        for i, x in enumerate((k, v)):
            n = 2 * step + i
            copies.append(
                pltpu.make_async_copy(x.at[:, pl.ds(step * W, W)], rows.at[:, pl.ds(n * W, W)], sems.at[n])
            )
            copies[-1].start()
    for part in range(3):
        c = slice(part * 4 * W, part * 4 * W + 4 * W)
        for copy in copies[4 * part : 4 * part + 4]:
            copy.wait()
        x1 = fold(rows[:, c])
        x2 = fold(x1)
        l12[:128, c] = x1
        l12[128:, c] = x2
        l3[:, c] = fold(x2)


def pyramid(k, v):
    far = pl.BlockSpec(memory_space=pl.ANY)
    near = pl.BlockSpec(memory_space=pltpu.VMEM)
    return pl.pallas_call(
        pyramid_kernel,
        in_specs=[far, far],
        out_specs=[near, near],
        out_shape=shapes(((192, PAIR), BF), ((32, PAIR), BF)),
        scratch_shapes=[pltpu.VMEM((T, PAIR), BF), pltpu.SemaphoreType.DMA((2 * STEPS,))],
        cost_estimate=cost(1.9),
        compiler_params=params(10),
        name="pyramid",
    )(k, v)


def chip_kernel(mine, other, l4, l5):
    x = fold(jnp.concatenate([mine[...], other[...]], 0))
    l4[...] = x
    l5[...] = fold(x)


def row_kernel(l5, z1, z2, z3, l6, l7):
    x = fold(jnp.concatenate([l5[...], fold(z1[...]), z2[...], z3[...]], 0))
    l6[...] = x
    l7[...] = fold(x)


def head(q, k0, v0, k12, v12, xk, xv, ga, bias, expand):
    s_all = mm(jnp.concatenate([k0, k12, xk], 0), q, NT)
    g_all = mm(jnp.concatenate([v0, v12, xv], 0), ga, NT)
    low = lax.broadcasted_iota(jnp.int32, (1, 128), 1) < 64
    low64 = jnp.broadcast_to(low, (64, 128))
    low32 = low64[:32]

    def pick(full, j):
        c = full[:, 128 * j : 128 * j + 128]
        a = jnp.where(low, c[128 * j : 128 * j + 64], c[128 * j + 64 : 128 * j + 128])
        b = jnp.where(low, c[288 + 64 * j : 320 + 64 * j], c[256 + 64 * j : 288 + 64 * j])
        d = c[416 - 32 * j : 448 - 32 * j]
        return jnp.concatenate([a, b, d, c[448:608]], 0)

    def widen(x):
        a, b = x[:64], x[64:96]
        za, zb = jnp.zeros_like(a), jnp.zeros_like(b)
        return jnp.concatenate(
            [
                jnp.where(low64, a, za),
                jnp.where(low64, za, a),
                jnp.where(low32, zb, b),
                jnp.where(low32, b, zb),
                x[96:],
            ],
            0,
        )

    att, gq, g0, g1, g2, px, sx = [], [], [], [], [None, None], [], []
    for j in range(2):
        s = pick(s_all, j) * SCALE + bias
        e = jnp.exp(s - jnp.max(s, axis=0, keepdims=True))
        p = e * (1.0 / jnp.sum(e, axis=0, keepdims=True))
        pb = p.astype(BF)
        gp = pick(g_all, j)
        delta = jnp.sum(pb.astype(F) * gp, axis=0, keepdims=True)
        gs = (p * (gp - delta) * SCALE).astype(BF)
        pw, sw = widen(pb), widen(gs)
        rows, o = slice(128 * j, 128 * j + 128), 1 - j
        near = slice(64 * j, 64 * j + 64)
        far = slice(128 + 32 * o, 160 + 32 * o)
        kh = jnp.concatenate([k0[rows], k12[near], k12[far], xk], 0)
        vh = jnp.concatenate([v0[rows], v12[near], v12[far], xv], 0)
        att.append(mm(pw, vh, TN))
        gq.append(mm(sw, kh, TN))
        both = jnp.concatenate([mm(sw[:224], q[rows], NN), mm(pw[:224], ga[rows], NN)], 1)
        g0.append(both[:128])
        g1.append(both[128:192])
        g2[o] = both[192:224]
        px.append(pw[224:])
        sx.append(sw[224:])
    gxk = mm(jnp.concatenate(sx, 1), q, NN)
    gxv = mm(jnp.concatenate(px, 1), ga, NN)
    coarse = jnp.concatenate(g1 + g2, 0).astype(BF)
    fine = jnp.concatenate(g0, 0) + mm(expand, coarse, NN)
    return jnp.concatenate(att, 0), jnp.concatenate(gq, 0), fine, gxk, gxv


def lanes(n, wide):
    return pl.ds(pl.multiple_of(n * wide, wide), wide)


def attention_kernel(bits, q, k, v, l12, c1, z1, z2, z3, y1, y2, y3, ga, *rest, first):
    if first:
        att_o, gq_o, fine_o, near_o, far_o, attt_o = rest
    else:
        far_i, att_o, gq_o, fine_o, near_o, gy1_o, gy2_o, gy3_o, attt_o = rest
        for out, rows in ((gy1_o, slice(0, 32)), (gy2_o, slice(32, 48)), (gy3_o, slice(48, 64))):
            out[:, :D] = far_i[rows, :]
    base = (1 - bits[XH] if first else bits[XH]) * HALF_STEPS
    r = lax.broadcasted_iota(jnp.int32, (T, 192), 0)
    c = lax.broadcasted_iota(jnp.int32, (T, 192), 1)
    half = jnp.where((r >> 1) == c, 0.5, 0.0)
    expand = jnp.where(c < 128, half, jnp.where((r >> 2) == c - 128, 0.25, 0.0)).astype(BF)
    r = lax.broadcasted_iota(jnp.int32, (288, 1), 0)
    bias = jnp.where(r < 64, 0, (r >> 5) - 1).astype(F) * LN2

    def step(i, carry):
        wide, pair = lanes(base + i, W), lanes(base + i, 2 * W)
        qs, ks, vs, gas, ps = q[:, wide], k[:, wide], v[:, wide], ga[:, wide], l12[:, pair]
        x = jnp.concatenate([p[:, pair] for p in (c1, z1, z2, z3, y1, y2, y3)], 0)
        done = []
        for h in range(HS):
            a = slice(h * HD, h * HD + HD)
            b = slice(W + h * HD, W + h * HD + HD)
            done.append(
                head(qs[:, a], ks[:, a], vs[:, a], ps[:, a], ps[:, b], x[:, a], x[:, b], gas[:, a], bias, expand)
            )
        att = jnp.concatenate([d[0] for d in done], 1)
        att_o[:, lanes(i, W)] = att.astype(BF)
        attt_o[lanes(i, W), :] = jnp.transpose(att).astype(BF)
        gq_o[:, lanes(i, W)] = jnp.concatenate([d[1] for d in done], 1).astype(BF)
        parts = [d[2][:, :HD] for d in done] + [d[2][:, HD:] for d in done]
        fine_o[:, lanes(i, 2 * W)] = jnp.concatenate(parts, 1)
        g = jnp.concatenate([d[3] for d in done] + [d[4] for d in done], 1)
        near_o[:, lanes(i, 2 * W)] = g[:96]
        gb = g[96:].astype(BF)
        if first:
            far_o[:, lanes(i, 2 * W)] = gb
        else:
            to = lanes(i + HALF_STEPS, 2 * W)
            gy1_o[:, to] = gb[:32]
            gy2_o[:, to] = gb[32:48]
            gy3_o[:, to] = gb[48:]
        return carry

    lax.fori_loop(0, HALF_STEPS, step, 0, unroll=UNROLL)


def attention(bits, q, k, v, l12, pieces, ga, *far):
    first = not far
    outs = [((T, D // 2), BF), ((T, D // 2), BF), ((T, D), F), ((96, D), F)]
    outs += [((64, D), BF)] if first else [((32, PAIR), BF), ((16, PAIR), BF), ((16, PAIR), BF)]
    outs += [((D // 2, T), BF)]
    return placed(
        lambda *refs: attention_kernel(*refs, first=first), outs, "attention", 7, 32, bits, q, k, v, l12, *pieces, ga, *far
    )


def placed(kernel, outs, name, us, mib, bits, *operands):
    vmem = pl.BlockSpec(memory_space=pltpu.VMEM)
    return pl.pallas_call(
        kernel,
        in_specs=[pl.BlockSpec(memory_space=pltpu.SMEM)] + [vmem] * len(operands),
        out_specs=[vmem] * len(outs),
        out_shape=shapes(*outs),
        cost_estimate=cost(us),
        compiler_params=params(mib),
        name=name,
    )(bits, *operands)


def back_row_kernel(near_a, near_b, y1, y2, y3, s1, s2, s3, own):
    g6 = y1[...].astype(F) + spread(y2[...].astype(F) + y3[...].astype(F), 1)
    for i, near in enumerate((near_a, near_b)):
        c = slice(i * D, i * D + D)
        s1[:, c] = (near[32:64, :] + spread(g6[8:16, c], 2)).astype(BF)
        s2[:, c] = (near[64:80, :] + spread(g6[16:24, c], 1)).astype(BF)
        s3[:, c] = (near[80:, :] + spread(g6[24:, c], 1)).astype(BF)
    own[...] = spread(g6[:8], 2)


def back_chip_kernel(near_a, near_b, own, z1, z2, z3, send, keep):
    g4 = own[...] + z1[...].astype(F) + spread(z2[...].astype(F) + z3[...].astype(F), 1)
    for i, near in enumerate((near_a, near_b)):
        c = slice(i * D, i * D + D)
        send[:, c] = (near[:32, :] + spread(g4[16:, c], 1)).astype(BF)
    keep[...] = spread(g4[:16], 1)


def finish_kernel(bits, fine_a, fine_b, keep, c1, gk, gv):
    g3 = spread(keep[...] + c1[...].astype(F), 3)
    for half, (fine, side) in enumerate(((fine_a, 1 - bits[XH]), (fine_b, bits[XH]))):
        for step in range(HALF_STEPS):
            for i, out in enumerate((gk, gv)):
                n = 2 * step + i
                total = fine[:, n * W : n * W + W] + g3[:, half * D + n * W : half * D + n * W + W]
                out[:, lanes(side * HALF_STEPS + step, W)] = total.astype(BF)


def split_kernel(bits, go, go_m, go_o):
    mine = bits[CORE]
    half = D // 2
    go_m[...] = go[:, pl.ds(pl.multiple_of(mine * half, half), half)]
    go_o[...] = go[:, pl.ds(pl.multiple_of((1 - mine) * half, half), half)]


def split(bits, go):
    vmem = pl.BlockSpec(memory_space=pltpu.VMEM)
    return pl.pallas_call(
        split_kernel,
        in_specs=[pl.BlockSpec(memory_space=pltpu.SMEM), vmem],
        out_specs=[vmem] * 2,
        out_shape=shapes(*[((T, D // 2), BF)] * 2),
        cost_estimate=cost(0.3),
        compiler_params=params(10),
        name="split",
    )(bits, go)


def grad_attended_kernel(go, w, ga):
    for c in range(0, D, 256):
        ga[:, c : c + 256] = mm(go[...], w[c : c + 256, :], NT).astype(BF)


def mixed_kernel(bits, att_a, att_b, gq_a, gq_b, w, mixed, gq):
    half = D // 2
    a, b = lanes(1 - bits[XH], half), lanes(bits[XH], half)
    gq[:, a] = gq_a[...]
    gq[:, b] = gq_b[...]
    for c in range(0, D, 256):
        cols = slice(c, c + 256)
        mixed[:, cols] = (mm(att_a[...], w[a, cols], NN) + mm(att_b[...], w[b, cols], NN)).astype(BF)


def small(kernel, outs, name, us=0.4):
    return pl.pallas_call(kernel, out_shape=shapes(*outs), cost_estimate=cost(us),
        compiler_params=params(12), name=name)


def halves(which, outer, half):
    for o in range(outer):
        first = pl.multiple_of((2 * o + which) * half, 16 if half % 16 == 0 else 8)
        yield slice(o * half, o * half + half), pl.ds(first, half)


def weight_kernel(bits, *refs, color, bit, outer, half):
    send, keep = refs[-2:]
    n = (len(refs) - 2) // 2
    atts, gos = refs[:n], refs[n : 2 * n]
    away = 1 - bits[bit]
    c = slice(color * PART, color * PART + PART)
    for out, which in ((send, away), (keep, 1 - away)):
        for to, rows in halves(which, outer, half):
            out[to, :] = sum(mm(a[rows, :], g[:, c], NN) for a, g in zip(atts, gos, strict=True)).astype(BF)


def weight(bits, atts, gos, color, bit, outer, half):
    vmem = pl.BlockSpec(memory_space=pltpu.VMEM)
    return pl.pallas_call(
        lambda *refs: weight_kernel(*refs, color=color, bit=bit, outer=outer, half=half),
        in_specs=[pl.BlockSpec(memory_space=pltpu.SMEM)] + [vmem] * (2 * len(atts)),
        out_specs=[vmem, vmem],
        out_shape=shapes(((D // 4, PART), BF), ((D // 4, PART), BF)),
        cost_estimate=cost(1.5),
        compiler_params=params(10),
        name="weight_part",
    )(bits, *atts, *gos)


def merge_kernel(bits, *refs, bit, outer, half):
    away = 1 - bits[bit]
    n = (len(refs) - 2) // 2
    for out, which in ((refs[-2], away), (refs[-1], 1 - away)):
        for to, rows in halves(which, outer, half):
            for i in range(n):
                a, b = refs[2 * i], refs[2 * i + 1]
                w = a.shape[1]
                s = a[rows, :].astype(F) + b[rows, :].astype(F)
                out[to, i * w : i * w + w] = s.astype(out.dtype)


def merge(bits, pairs, bit, outer, half, dtype=BF):
    operands = [x for pair in pairs for x in pair]
    wide = sum(pair[0].shape[1] for pair in pairs)
    vmem = pl.BlockSpec(memory_space=pltpu.VMEM)
    return pl.pallas_call(
        lambda *refs: merge_kernel(*refs, bit=bit, outer=outer, half=half),
        in_specs=[pl.BlockSpec(memory_space=pltpu.SMEM)] + [vmem] * len(operands),
        out_specs=[vmem, vmem],
        out_shape=shapes(*[((outer * half, wide), dtype)] * 2),
        cost_estimate=cost(0.6),
        compiler_params=params(10),
        name="merge",
    )(bits, *operands)


def last_merge_kernel(bits, a_k, a_r, b_k, b_r, *outs):
    y, z = bits[YL], bits[ZL]
    total = jnp.concatenate(
        [a_k[...].astype(F) + a_r[...].astype(F), b_k[...].astype(F) + b_r[...].astype(F)], 1
    )
    quarters = [total[24 * i : 24 * i + 24] for i in range(4)]
    for out, dy, dz in zip(outs, (1, 0, 1, 0), (0, 1, 1, 0), strict=True):
        low = [jnp.where((z ^ dz) == 0, quarters[2 * i], quarters[2 * i + 1]) for i in range(2)]
        out[...] = jnp.where((y ^ dy) == 0, low[0], low[1])


def last_merge(bits, *operands):
    vmem = pl.BlockSpec(memory_space=pltpu.VMEM)
    return pl.pallas_call(
        last_merge_kernel,
        in_specs=[pl.BlockSpec(memory_space=pltpu.SMEM)] + [vmem] * 4,
        out_specs=[vmem] * 4,
        out_shape=shapes(*[((24, D // 2), F)] * 4),
        cost_estimate=cost(0.6),
        compiler_params=params(10),
        name="last_merge",
    )(bits, *operands)


def after(x, *others):
    return lax.optimization_barrier((x, *others))[0]


def across(x, flip):
    return lax.ppermute(x, "seq", [(i, i ^ flip) for i in range(32)])


def across_x(x, flip):
    return lax.ppermute(x, "dp", [(i, i ^ flip) for i in range(4)])


XH, XL, YH, YL, ZH, ZL, CORE = range(7)


def local(query, key, value, w_out, grad_out):
    q, k, v, go = query[0], key[0], value[0], grad_out[0]
    place = lax.axis_index("seq")
    row = lax.axis_index("dp")
    core = place & 1
    bits = jnp.stack(
        [row >> 1, row & 1, place >> 4 & 1, place >> 3 & 1, place >> 2 & 1, place >> 1 & 1, core]
    ).astype(jnp.int32)
    l12, l3 = pyramid(after(k, bits), v)
    c1 = across(l3, 1)
    l4, l5 = small(chip_kernel, [((32, PAIR), BF), ((16, PAIR), BF)], "chip")(l3, c1)
    z1, z3, z2 = across(l4, 2), across(l5, 6), across(l5, 4)
    go_m, go_s = split(bits, after(go, l3))
    go_o = across(go_s, 1)
    l5 = after(l5, go_o)
    ga = small(grad_attended_kernel, [((T, D), BF)], "grad_attended", 2.0)(after(go, z1), w_out)[0]
    l6, l7 = small(row_kernel, [((32, PAIR), BF), ((16, PAIR), BF)], "row")(l5, z1, z2, z3)
    gox_m, gox_o = across_x(go_m, 3), across_x(go_o, 3)
    y1, y3, y2 = across(l6, 8), across(l7, 24), across(l7, 16)
    pieces = (c1, z1, z2, z3, y1, y2, y3)
    att_a, gq_a, fine_a, near_a, far, sent = attention(bits, after(q, gox_m, gox_o), k, v, l12, pieces, ga)
    att_x = across_x(sent, 3)
    att_b, gq_b, fine_b, near_b, gy1, gy2, gy3, att_m = attention(
        bits, after(q, sent), k, v, l12, pieces, ga, far
    )
    att_o, att_xo = across(att_m, 1), across(att_x, 1)
    y1, y3, y2 = across(gy1, 8), across(gy3, 24), across(gy2, 16)
    atts = (att_m, att_o, att_x, att_xo)
    gos = (go_m, go_o, gox_m, gox_o)
    b_s, b_k = weight(bits, atts, gos, 1, ZH, 8, 48)
    b_r = across(b_s, 6)
    a_s, a_k = weight(bits, (after(att_m, b_k), *atts[1:]), gos, 0, XL, 1, 384)
    a_r = across_x(a_s, 1)
    s1, s2, s3, own = small(
        back_row_kernel, [((32, PAIR), BF), ((16, PAIR), BF), ((16, PAIR), BF), ((32, PAIR), F)], "back_row"
    )(near_a, after(near_b, a_k), y1, y2, y3)
    z1, z3, z2 = across(s1, 2), across(s3, 6), across(s2, 4)
    b_s, b_k = merge(bits, [(after(b_k, own), b_r)], YH, 2, 96)
    b_r = across(b_s, 24)
    a_s, a_k = merge(bits, [(after(a_k, b_k), a_r)], ZH, 4, 48)
    a_r = across(a_s, 6)
    mixed, gq = placed(
        mixed_kernel, [((T, D), BF)] * 2, "mixed", 2.3, 12, bits, after(att_a, a_k), att_b, gq_a, gq_b, w_out
    )
    send, keep = small(back_chip_kernel, [((32, PAIR), BF), ((32, PAIR), F)], "back_chip")(
        near_a, after(near_b, mixed), own, z1, z2, z3
    )
    c1 = across(send, 1)
    b_s, b_k = merge(bits, [(after(b_k, keep), b_r)], XL, 1, 96)
    b_r = across_x(b_s, 1)
    a_s, a_k = merge(bits, [(after(a_k, b_k), a_r)], YH, 1, 96)
    a_r = across(a_s, 24)
    gk, gv = placed(
        finish_kernel, [((T, D), BF)] * 2, "finish", 1.7, 12, bits, after(fine_a, a_k), fine_b, keep, c1
    )
    s1, s2, s3, kept = last_merge(bits, after(a_k, gk), a_r, b_k, b_r)
    part = kept + across(s1, 8) + across(s2, 2) + across(s3, 10)
    first = core == 0
    mine = jnp.where(first, part[:12], part[12:])
    theirs = across(jnp.where(first, part[12:], part[:12]), 1)
    total = jnp.concatenate([jnp.where(first, mine, theirs), jnp.where(first, theirs, mine)], 1)
    gw = total * (1.0 / math.sqrt(4 * 32 * T))
    return mixed[None], gq[None], gk[None], gv[None], gw


def solution(mesh):
    rows = P("dp", "seq", None)
    return jax.shard_map(
        local,
        mesh=mesh,
        in_specs=(rows, rows, rows, P(), rows),
        out_specs=(rows, rows, rows, rows, P(("dp", "seq"), None)),
        check_vma=False,
    )
```

```python
import math

import jax
import jax.numpy as jnp
from jax import lax
from jax.experimental import pallas as pl
from jax.experimental.pallas import tpu as pltpu
from jax.sharding import PartitionSpec as P

H = 12
HD = 128
D = 1536
T = 256
HS = 2
W = HS * HD
STEPS = H // HS
HALF_STEPS = STEPS // 2
UNROLL = True
BF = jnp.bfloat16
F = jnp.float32
NT = (((1,), (1,)), ((), ()))
TN = (((0,), (0,)), ((), ()))
NN = (((1,), (0,)), ((), ()))
LN2 = math.log(2.0)
SCALE = HD**-0.5
PART = D // 4
PAIR = 2 * D


def mm(a, b, dims):
    return lax.dot_general(a, b, dims, preferred_element_type=F)


def params(mib):
    return pltpu.CompilerParams(vmem_limit_bytes=mib * 2**20)


def cost(us):
    return pl.CostEstimate(flops=0, bytes_accessed=int(us * 3.7e6), transcendentals=0)


def shapes(*items):
    return [jax.ShapeDtypeStruct(s, t) for s, t in items]


def fold_matrix(n):
    r = lax.broadcasted_iota(jnp.int32, (n, 2 * n), 0)
    c = lax.broadcasted_iota(jnp.int32, (n, 2 * n), 1)
    return jnp.where((c >> 1) == r, 0.5, 0.0).astype(BF)


def fold(x):
    return mm(fold_matrix(x.shape[0] // 2), x, NN).astype(BF)


def spread(x, bits):
    n = x.shape[0]
    r = lax.broadcasted_iota(jnp.int32, (n << bits, n), 0)
    c = lax.broadcasted_iota(jnp.int32, (n << bits, n), 1)
    return mm(jnp.where((r >> bits) == c, 0.5**bits, 0.0).astype(BF), x.astype(BF), NN)


def means_of(x):
    r = lax.broadcasted_iota(jnp.int32, (224, T), 0)
    c = lax.broadcasted_iota(jnp.int32, (224, T), 1)
    low = jnp.where(r < 192, jnp.where((c >> 2) == r - 128, 0.25, 0.0), jnp.where((c >> 3) == r - 192, 0.125, 0.0))
    means = jnp.where(r < 128, jnp.where((c >> 1) == r, 0.5, 0.0), low).astype(BF)
    return [mm(means, x[:, n * W : n * W + W], NN).astype(BF) for n in range(STEPS)]


def key_means_kernel(k, l12, l3):
    for n, x in enumerate(means_of(k)):
        l12[:, n * W : n * W + W] = x[:192]
        l3[:, n * W : n * W + W] = x[192:]


def value_means_kernel(v, l3_k, l12, l3):
    for n, x in enumerate(means_of(v)):
        l12[:, n * W : n * W + W] = x[:192]
        l3[:, 2 * n * W : (2 * n + 1) * W] = l3_k[:, n * W : n * W + W]
        l3[:, (2 * n + 1) * W : (2 * n + 2) * W] = x[192:]


def chip_kernel(mine, other, l4, l5):
    x = fold(jnp.concatenate([mine[...], other[...]], 0))
    l4[...] = x
    l5[...] = fold(x)


def row_kernel(l5, z1, z2, z3, l6, l7):
    x = fold(jnp.concatenate([l5[...], fold(z1[...]), z2[...], z3[...]], 0))
    l6[...] = x
    l7[...] = fold(x)


def head(q, k0, v0, k12, v12, xk, xv, ga, bias, expand):
    s_all = mm(jnp.concatenate([k0, k12, xk], 0), q, NT)
    g_all = mm(jnp.concatenate([v0, v12, xv], 0), ga, NT)
    low = lax.broadcasted_iota(jnp.int32, (1, 128), 1) < 64
    low64 = jnp.broadcast_to(low, (64, 128))
    low32 = low64[:32]

    def pick(full, j):
        c = full[:, 128 * j : 128 * j + 128]
        a = jnp.where(low, c[128 * j : 128 * j + 64], c[128 * j + 64 : 128 * j + 128])
        b = jnp.where(low, c[288 + 64 * j : 320 + 64 * j], c[256 + 64 * j : 288 + 64 * j])
        d = c[416 - 32 * j : 448 - 32 * j]
        return jnp.concatenate([a, b, d, c[448:608]], 0)

    def widen(x):
        a, b = x[:64], x[64:96]
        za, zb = jnp.zeros_like(a), jnp.zeros_like(b)
        return jnp.concatenate(
            [
                jnp.where(low64, a, za),
                jnp.where(low64, za, a),
                jnp.where(low32, zb, b),
                jnp.where(low32, b, zb),
                x[96:],
            ],
            0,
        )

    att, gq, g0, g1, g2, px, sx = [], [], [], [], [None, None], [], []
    for j in range(2):
        s = pick(s_all, j) * SCALE + bias
        e = jnp.exp(s - jnp.max(s, axis=0, keepdims=True))
        p = e * (1.0 / jnp.sum(e, axis=0, keepdims=True))
        pb = p.astype(BF)
        gp = pick(g_all, j)
        delta = jnp.sum(pb.astype(F) * gp, axis=0, keepdims=True)
        gs = (p * (gp - delta) * SCALE).astype(BF)
        pw, sw = widen(pb), widen(gs)
        rows, o = slice(128 * j, 128 * j + 128), 1 - j
        near = slice(64 * j, 64 * j + 64)
        far = slice(128 + 32 * o, 160 + 32 * o)
        kh = jnp.concatenate([k0[rows], k12[near], k12[far], xk], 0)
        vh = jnp.concatenate([v0[rows], v12[near], v12[far], xv], 0)
        att.append(mm(pw, vh, TN))
        gq.append(mm(sw, kh, TN))
        both = jnp.concatenate([mm(sw[:224], q[rows], NN), mm(pw[:224], ga[rows], NN)], 1)
        g0.append(both[:128])
        g1.append(both[128:192])
        g2[o] = both[192:224]
        px.append(pw[224:])
        sx.append(sw[224:])
    gxk = mm(jnp.concatenate(sx, 1), q, NN)
    gxv = mm(jnp.concatenate(px, 1), ga, NN)
    coarse = jnp.concatenate(g1 + g2, 0).astype(BF)
    fine = jnp.concatenate(g0, 0) + mm(expand, coarse, NN)
    return jnp.concatenate(att, 0), jnp.concatenate(gq, 0), fine, gxk, gxv


def lanes(n, wide):
    return pl.ds(pl.multiple_of(n * wide, wide), wide)


def attention_kernel(bits, q, k, v, k12, v12, c1, z1, z2, z3, y1, y2, y3, ga, *rest, first):
    if first:
        att_o, gq_o, fine_o, near_o, far_o, attt_o = rest
    else:
        far_i, att_o, gq_o, fine_o, near_o, gy1_o, gy2_o, gy3_o, attt_o = rest
        for out, rows in ((gy1_o, slice(0, 32)), (gy2_o, slice(32, 48)), (gy3_o, slice(48, 64))):
            out[:, :D] = far_i[rows, :]
    base = (1 - bits[XH] if first else bits[XH]) * HALF_STEPS
    r = lax.broadcasted_iota(jnp.int32, (T, 192), 0)
    c = lax.broadcasted_iota(jnp.int32, (T, 192), 1)
    half = jnp.where((r >> 1) == c, 0.5, 0.0)
    expand = jnp.where(c < 128, half, jnp.where((r >> 2) == c - 128, 0.25, 0.0)).astype(BF)
    r = lax.broadcasted_iota(jnp.int32, (288, 1), 0)
    bias = jnp.where(r < 64, 0, (r >> 5) - 1).astype(F) * LN2

    def step(i, carry):
        wide, pair = lanes(base + i, W), lanes(base + i, 2 * W)
        qs, ks, vs, gas = q[:, wide], k[:, wide], v[:, wide], ga[:, wide]
        kps, vps = k12[:, wide], v12[:, wide]
        x = jnp.concatenate([p[:, pair] for p in (c1, z1, z2, z3, y1, y2, y3)], 0)
        done = []
        for h in range(HS):
            a = slice(h * HD, h * HD + HD)
            b = slice(W + h * HD, W + h * HD + HD)
            done.append(
                head(qs[:, a], ks[:, a], vs[:, a], kps[:, a], vps[:, a], x[:, a], x[:, b], gas[:, a], bias, expand)
            )
        att = jnp.concatenate([d[0] for d in done], 1)
        att_o[:, lanes(i, W)] = att.astype(BF)
        attt_o[lanes(i, W), :] = jnp.transpose(att).astype(BF)
        gq_o[:, lanes(i, W)] = jnp.concatenate([d[1] for d in done], 1).astype(BF)
        parts = [d[2][:, :HD] for d in done] + [d[2][:, HD:] for d in done]
        fine_o[:, lanes(i, 2 * W)] = jnp.concatenate(parts, 1)
        g = jnp.concatenate([d[3] for d in done] + [d[4] for d in done], 1)
        near_o[:, lanes(i, 2 * W)] = g[:96]
        gb = g[96:].astype(BF)
        if first:
            far_o[:, lanes(i, 2 * W)] = gb
        else:
            to = lanes(i + HALF_STEPS, 2 * W)
            gy1_o[:, to] = gb[:32]
            gy2_o[:, to] = gb[32:48]
            gy3_o[:, to] = gb[48:]
        return carry

    lax.fori_loop(0, HALF_STEPS, step, 0, unroll=UNROLL)


def attention(bits, q, k, v, k12, v12, pieces, ga, *far):
    first = not far
    outs = [((T, D // 2), BF), ((T, D // 2), BF), ((T, D), F), ((96, D), F)]
    outs += [((64, D), BF)] if first else [((32, PAIR), BF), ((16, PAIR), BF), ((16, PAIR), BF)]
    outs += [((D // 2, T), BF)]
    return placed(
        lambda *refs: attention_kernel(*refs, first=first), outs, "attention", 7, 32, bits, q, k, v, k12, v12, *pieces, ga, *far
    )


def placed(kernel, outs, name, us, mib, bits, *operands):
    vmem = pl.BlockSpec(memory_space=pltpu.VMEM)
    return pl.pallas_call(
        kernel,
        in_specs=[pl.BlockSpec(memory_space=pltpu.SMEM)] + [vmem] * len(operands),
        out_specs=[vmem] * len(outs),
        out_shape=shapes(*outs),
        cost_estimate=cost(us),
        compiler_params=params(mib),
        name=name,
    )(bits, *operands)


def back_row_kernel(near_a, near_b, y1, y2, y3, s1, s2, s3, own):
    g6 = y1[...].astype(F) + spread(y2[...].astype(F) + y3[...].astype(F), 1)
    for i, near in enumerate((near_a, near_b)):
        c = slice(i * D, i * D + D)
        s1[:, c] = (near[32:64, :] + spread(g6[8:16, c], 2)).astype(BF)
        s2[:, c] = (near[64:80, :] + spread(g6[16:24, c], 1)).astype(BF)
        s3[:, c] = (near[80:, :] + spread(g6[24:, c], 1)).astype(BF)
    own[...] = spread(g6[:8], 2)


def back_chip_kernel(near_a, near_b, own, z1, z2, z3, send, keep):
    g4 = own[...] + z1[...].astype(F) + spread(z2[...].astype(F) + z3[...].astype(F), 1)
    for i, near in enumerate((near_a, near_b)):
        c = slice(i * D, i * D + D)
        send[:, c] = (near[:32, :] + spread(g4[16:, c], 1)).astype(BF)
    keep[...] = spread(g4[:16], 1)


def finish_kernel(bits, fine_a, fine_b, keep, c1, gk, gv):
    g3 = spread(keep[...] + c1[...].astype(F), 3)
    for half, (fine, side) in enumerate(((fine_a, 1 - bits[XH]), (fine_b, bits[XH]))):
        for step in range(HALF_STEPS):
            for i, out in enumerate((gk, gv)):
                n = 2 * step + i
                total = fine[:, n * W : n * W + W] + g3[:, half * D + n * W : half * D + n * W + W]
                out[:, lanes(side * HALF_STEPS + step, W)] = total.astype(BF)


def split_kernel(bits, go, go_m, go_o):
    mine = bits[CORE]
    half = D // 2
    go_m[...] = go[:, pl.ds(pl.multiple_of(mine * half, half), half)]
    go_o[...] = go[:, pl.ds(pl.multiple_of((1 - mine) * half, half), half)]


def split(bits, go):
    vmem = pl.BlockSpec(memory_space=pltpu.VMEM)
    return pl.pallas_call(
        split_kernel,
        in_specs=[pl.BlockSpec(memory_space=pltpu.SMEM), vmem],
        out_specs=[vmem] * 2,
        out_shape=shapes(*[((T, D // 2), BF)] * 2),
        cost_estimate=cost(0.3),
        compiler_params=params(10),
        name="split",
    )(bits, go)


def grad_attended_kernel(go, w, ga):
    for c in range(0, D, 256):
        ga[:, c : c + 256] = mm(go[...], w[c : c + 256, :], NT).astype(BF)


def mixed_kernel(bits, att_a, att_b, w, mixed):
    half = D // 2
    a, b = lanes(1 - bits[XH], half), lanes(bits[XH], half)
    for c in range(0, D, 256):
        cols = slice(c, c + 256)
        mixed[:, cols] = (mm(att_a[...], w[a, cols], NN) + mm(att_b[...], w[b, cols], NN)).astype(BF)


def join_kernel(bits, gq_a, gq_b, gq):
    half = D // 2
    gq[:, lanes(1 - bits[XH], half)] = gq_a[...]
    gq[:, lanes(bits[XH], half)] = gq_b[...]


def small(kernel, outs, name, us=0.4):
    return pl.pallas_call(kernel, out_shape=shapes(*outs), cost_estimate=cost(us),
        compiler_params=params(12), name=name)


def halves(which, outer, half):
    for o in range(outer):
        first = pl.multiple_of((2 * o + which) * half, 16 if half % 16 == 0 else 8)
        yield slice(o * half, o * half + half), pl.ds(first, half)


def weight_kernel(bits, *refs, color, bit, outer, half):
    atts, gos, (send, keep, whole) = refs[:4], refs[4:8], refs[8:]
    c = slice(color * PART, color * PART + PART)
    for rows in range(0, D // 2, 384):
        r = slice(rows, rows + 384)
        whole[r, :] = sum(mm(a[r, :], g[:, c], NN) for a, g in zip(atts, gos, strict=True)).astype(BF)
    away = 1 - bits[bit]
    for out, which in ((send, away), (keep, 1 - away)):
        for to, rows in halves(which, outer, half):
            out[to, :] = whole[rows, :]


def weight(bits, atts, gos, color, bit, outer, half):
    vmem = pl.BlockSpec(memory_space=pltpu.VMEM)
    return pl.pallas_call(
        lambda *refs: weight_kernel(*refs, color=color, bit=bit, outer=outer, half=half),
        in_specs=[pl.BlockSpec(memory_space=pltpu.SMEM)] + [vmem] * (2 * len(atts)),
        out_specs=[vmem, vmem],
        out_shape=shapes(((D // 4, PART), BF), ((D // 4, PART), BF)),
        scratch_shapes=[pltpu.VMEM((D // 2, PART), BF)],
        cost_estimate=cost(1.5),
        compiler_params=params(10),
        name="weight_part",
    )(bits, *atts, *gos)


def merge_kernel(bits, *refs, bit, outer, half):
    away = 1 - bits[bit]
    n = (len(refs) - 2) // 2
    for out, which in ((refs[-2], away), (refs[-1], 1 - away)):
        for to, rows in halves(which, outer, half):
            for i in range(n):
                a, b = refs[2 * i], refs[2 * i + 1]
                w = a.shape[1]
                s = a[rows, :].astype(F) + b[rows, :].astype(F)
                out[to, i * w : i * w + w] = s.astype(out.dtype)


def merge(bits, pairs, bit, outer, half, dtype=BF):
    operands = [x for pair in pairs for x in pair]
    wide = sum(pair[0].shape[1] for pair in pairs)
    vmem = pl.BlockSpec(memory_space=pltpu.VMEM)
    return pl.pallas_call(
        lambda *refs: merge_kernel(*refs, bit=bit, outer=outer, half=half),
        in_specs=[pl.BlockSpec(memory_space=pltpu.SMEM)] + [vmem] * len(operands),
        out_specs=[vmem, vmem],
        out_shape=shapes(*[((outer * half, wide), dtype)] * 2),
        cost_estimate=cost(0.6),
        compiler_params=params(10),
        name="merge",
    )(bits, *operands)


def last_merge_kernel(bits, kept, got, *outs):
    y, z = bits[YL], bits[ZL]
    total = kept[...].astype(F) + got[...].astype(F)
    quarters = [total[24 * i : 24 * i + 24] for i in range(4)]
    for out, dy, dz in zip(outs, (1, 0, 1, 0), (0, 1, 1, 0), strict=True):
        low = [jnp.where((z ^ dz) == 0, quarters[2 * i], quarters[2 * i + 1]) for i in range(2)]
        out[...] = jnp.where((y ^ dy) == 0, low[0], low[1])


def last_merge(bits, *operands):
    vmem = pl.BlockSpec(memory_space=pltpu.VMEM)
    return pl.pallas_call(
        last_merge_kernel,
        in_specs=[pl.BlockSpec(memory_space=pltpu.SMEM)] + [vmem] * 2,
        out_specs=[vmem] * 4,
        out_shape=shapes(*[((24, D // 2), F)] * 4),
        cost_estimate=cost(0.6),
        compiler_params=params(10),
        name="last_merge",
    )(bits, *operands)


def tail_kernel(bits, kept, r1, r2, r3, mine, send):
    total = (kept[...] + r1[...]) + (r2[...] + r3[...])
    first = bits[CORE] == 0
    mine[...] = jnp.where(first, total[:12], total[12:])
    send[...] = jnp.where(first, total[12:], total[:12])


def after(x, *others):
    return lax.optimization_barrier((x, *others))[0]


def across(x, flip):
    return lax.ppermute(x, "seq", [(i, i ^ flip) for i in range(32)])


def across_x(x, flip):
    return lax.ppermute(x, "dp", [(i, i ^ flip) for i in range(4)])


XH, XL, YH, YL, ZH, ZL, CORE = range(7)


def local(query, key, value, w_out, grad_out):
    q, k, v, go = query[0], key[0], value[0], grad_out[0]
    place = lax.axis_index("seq")
    row = lax.axis_index("dp")
    core = place & 1
    bits = jnp.stack(
        [row >> 1, row & 1, place >> 4 & 1, place >> 3 & 1, place >> 2 & 1, place >> 1 & 1, core]
    ).astype(jnp.int32)
    k12, k3 = small(key_means_kernel, [((192, D), BF), ((32, D), BF)], "key_means")(after(k, bits))
    v12, l3 = small(value_means_kernel, [((192, D), BF), ((32, PAIR), BF)], "value_means")(v, k3)
    c1 = across(l3, 1)
    l4, l5 = small(chip_kernel, [((32, PAIR), BF), ((16, PAIR), BF)], "chip")(l3, c1)
    z1, z3, z2 = across(l4, 2), across(l5, 6), across(l5, 4)
    go_m, go_s = split(bits, after(go, l3))
    go_o = across(go_s, 1)
    l5 = after(l5, go_o)
    ga = small(grad_attended_kernel, [((T, D), BF)], "grad_attended", 2.0)(after(go, z1), w_out)[0]
    l6, l7 = small(row_kernel, [((32, PAIR), BF), ((16, PAIR), BF)], "row")(l5, z1, z2, z3)
    gox_m, gox_o = across_x(go_m, 3), across_x(go_o, 3)
    y1, y3, y2 = across(l6, 8), across(l7, 24), across(l7, 16)
    pieces = (c1, z1, z2, z3, y1, y2, y3)
    att_a, gq_a, fine_a, near_a, far, sent = attention(bits, after(q, gox_m, gox_o), k, v, k12, v12, pieces, ga)
    att_x = across_x(sent, 3)
    att_b, gq_b, fine_b, near_b, gy1, gy2, gy3, att_m = attention(
        bits, after(q, sent), k, v, k12, v12, pieces, ga, far
    )
    att_o, att_xo = across(att_m, 1), across(att_x, 1)
    y1, y3, y2 = across(gy1, 8), across(gy3, 24), across(gy2, 16)
    atts = (att_m, att_o, att_x, att_xo)
    gos = (go_m, go_o, gox_m, gox_o)
    b_s, b_k = weight(bits, (att_m, *atts[1:]), gos, 1, ZH, 8, 48)
    b_r = across(b_s, 6)
    a_s, a_k = weight(bits, (after(att_m, b_k), *atts[1:]), gos, 0, XL, 1, 384)
    a_r = across_x(a_s, 1)
    mixed = placed(mixed_kernel, [((T, D), BF)], "mixed", 2.3, 12, bits, after(att_a, a_k), att_b, w_out)[0]
    b_s, b_k = merge(bits, [(after(b_k, mixed), b_r)], XL, 1, 192)
    b_r = across_x(b_s, 1)
    a_s, a_k = merge(bits, [(after(a_k, b_k), a_r)], ZH, 4, 48)
    a_r = across(a_s, 6)
    s1, s2, s3, own = small(
        back_row_kernel, [((32, PAIR), BF), ((16, PAIR), BF), ((16, PAIR), BF), ((32, PAIR), F)], "back_row"
    )(near_a, after(near_b, a_k), y1, y2, y3)
    z1, z3, z2 = across(s1, 2), across(s3, 6), across(s2, 4)
    s, kept = merge(bits, [(after(a_k, own), a_r), (b_k, b_r)], YH, 1, 96)
    s_r = across(s, 24)
    gq = placed(join_kernel, [((T, D), BF)], "join", 0.7, 8, bits, after(gq_a, kept), gq_b)[0]
    send, keep = small(back_chip_kernel, [((32, PAIR), BF), ((32, PAIR), F)], "back_chip")(
        near_a, after(near_b, gq), own, z1, z2, z3
    )
    c1 = across(send, 1)
    s1, s2, s3, kept = last_merge(bits, after(kept, keep), s_r)
    r1, r2, r3 = across(s1, 8), across(s2, 2), across(s3, 10)
    gk, gv = placed(
        finish_kernel, [((T, D), BF)] * 2, "finish", 1.7, 12, bits, after(fine_a, kept), fine_b, keep, c1
    )
    mine, theirs = placed(tail_kernel, [((12, D // 2), F)] * 2, "tail", 0.4, 4, bits, after(kept, gk), r1, r2, r3)
    theirs = across(theirs, 1)
    first = core == 0
    total = jnp.concatenate([jnp.where(first, mine, theirs), jnp.where(first, theirs, mine)], 1)
    gw = total * (1.0 / math.sqrt(4 * 32 * T))
    return mixed[None], gq[None], gk[None], gv[None], gw


def solution(mesh):
    rows = P("dp", "seq", None)
    return jax.shard_map(
        local,
        mesh=mesh,
        in_specs=(rows, rows, rows, P(), rows),
        out_specs=(rows, rows, rows, rows, P(("dp", "seq"), None)),
        check_vma=False,
    )
```

```python
import math

import jax
import jax.numpy as jnp
from jax import lax
from jax.experimental import pallas as pl
from jax.experimental.pallas import tpu as pltpu
from jax.sharding import PartitionSpec as P

H = 12
HD = 128
D = 1536
T = 256
HS = 2
W = HS * HD
STEPS = H // HS
HALF_STEPS = STEPS // 2
UNROLL = True
BF = jnp.bfloat16
F = jnp.float32
NT = (((1,), (1,)), ((), ()))
TN = (((0,), (0,)), ((), ()))
NN = (((1,), (0,)), ((), ()))
LN2 = math.log(2.0)
SCALE = HD**-0.5
PART = D // 4
PAIR = 2 * D


XH, XL, YH, YL, ZH, ZL, CORE = range(7)


class Bits:
    def __getitem__(self, n):
        if n in (XH, XL):
            return lax.axis_index("dp") >> (1 - n) & 1
        return lax.axis_index("seq") >> (CORE - n) & 1


def mm(a, b, dims):
    return lax.dot_general(a, b, dims, preferred_element_type=F)


def params(mib):
    return pltpu.CompilerParams(vmem_limit_bytes=mib * 2**20)


def cost(us):
    return pl.CostEstimate(flops=0, bytes_accessed=int(us * 3.7e6), transcendentals=0)


def shapes(*items):
    return [jax.ShapeDtypeStruct(s, t) for s, t in items]


def fold_matrix(n):
    r = lax.broadcasted_iota(jnp.int32, (n, 2 * n), 0)
    c = lax.broadcasted_iota(jnp.int32, (n, 2 * n), 1)
    return jnp.where((c >> 1) == r, 0.5, 0.0).astype(BF)


def fold(x):
    return mm(fold_matrix(x.shape[0] // 2), x, NN).astype(BF)


def spread(x, bits):
    n = x.shape[0]
    r = lax.broadcasted_iota(jnp.int32, (n << bits, n), 0)
    c = lax.broadcasted_iota(jnp.int32, (n << bits, n), 1)
    return mm(jnp.where((r >> bits) == c, 0.5**bits, 0.0).astype(BF), x.astype(BF), NN)


def means_of(x):
    r = lax.broadcasted_iota(jnp.int32, (224, T), 0)
    c = lax.broadcasted_iota(jnp.int32, (224, T), 1)
    low = jnp.where(r < 192, jnp.where((c >> 2) == r - 128, 0.25, 0.0), jnp.where((c >> 3) == r - 192, 0.125, 0.0))
    means = jnp.where(r < 128, jnp.where((c >> 1) == r, 0.5, 0.0), low).astype(BF)
    return [mm(means, x[:, n * W : n * W + W], NN).astype(BF) for n in range(STEPS)]


def key_means_kernel(k, l12, l3):
    for n, x in enumerate(means_of(k)):
        l12[:, n * W : n * W + W] = x[:192]
        l3[:, n * W : n * W + W] = x[192:]


def value_means_kernel(v, l3_k, l12, l3):
    for n, x in enumerate(means_of(v)):
        l12[:, n * W : n * W + W] = x[:192]
        l3[:, 2 * n * W : (2 * n + 1) * W] = l3_k[:, n * W : n * W + W]
        l3[:, (2 * n + 1) * W : (2 * n + 2) * W] = x[192:]


def chip_kernel(mine, other, l4, l5):
    x = fold(jnp.concatenate([mine[...], other[...]], 0))
    l4[...] = x
    l5[...] = fold(x)


def row_kernel(l5, z1, z2, z3, l6, l7):
    x = fold(jnp.concatenate([l5[...], fold(z1[...]), z2[...], z3[...]], 0))
    l6[...] = x
    l7[...] = fold(x)


def head(q, k0, v0, k12, v12, xk, xv, ga, bias, expand):
    s_all = mm(jnp.concatenate([k0, k12, xk], 0), q, NT)
    g_all = mm(jnp.concatenate([v0, v12, xv], 0), ga, NT)
    low = lax.broadcasted_iota(jnp.int32, (1, 128), 1) < 64
    low64 = jnp.broadcast_to(low, (64, 128))
    low32 = low64[:32]

    def pick(full, j):
        c = full[:, 128 * j : 128 * j + 128]
        a = jnp.where(low, c[128 * j : 128 * j + 64], c[128 * j + 64 : 128 * j + 128])
        b = jnp.where(low, c[288 + 64 * j : 320 + 64 * j], c[256 + 64 * j : 288 + 64 * j])
        d = c[416 - 32 * j : 448 - 32 * j]
        return jnp.concatenate([a, b, d, c[448:608]], 0)

    def widen(x):
        a, b = x[:64], x[64:96]
        za, zb = jnp.zeros_like(a), jnp.zeros_like(b)
        return jnp.concatenate(
            [
                jnp.where(low64, a, za),
                jnp.where(low64, za, a),
                jnp.where(low32, zb, b),
                jnp.where(low32, b, zb),
                x[96:],
            ],
            0,
        )

    att, gq, g0, g1, g2, px, sx = [], [], [], [], [None, None], [], []
    for j in range(2):
        s = pick(s_all, j) * SCALE + bias
        e = jnp.exp(s - jnp.max(s, axis=0, keepdims=True))
        p = e * (1.0 / jnp.sum(e, axis=0, keepdims=True))
        pb = p.astype(BF)
        gp = pick(g_all, j)
        delta = jnp.sum(pb.astype(F) * gp, axis=0, keepdims=True)
        gs = (p * (gp - delta) * SCALE).astype(BF)
        pw, sw = widen(pb), widen(gs)
        rows, o = slice(128 * j, 128 * j + 128), 1 - j
        near = slice(64 * j, 64 * j + 64)
        far = slice(128 + 32 * o, 160 + 32 * o)
        kh = jnp.concatenate([k0[rows], k12[near], k12[far], xk], 0)
        vh = jnp.concatenate([v0[rows], v12[near], v12[far], xv], 0)
        att.append(mm(pw, vh, TN))
        gq.append(mm(sw, kh, TN))
        both = jnp.concatenate([mm(sw[:224], q[rows], NN), mm(pw[:224], ga[rows], NN)], 1)
        g0.append(both[:128])
        g1.append(both[128:192])
        g2[o] = both[192:224]
        px.append(pw[224:])
        sx.append(sw[224:])
    gxk = mm(jnp.concatenate(sx, 1), q, NN)
    gxv = mm(jnp.concatenate(px, 1), ga, NN)
    coarse = jnp.concatenate(g1 + g2, 0).astype(BF)
    fine = jnp.concatenate(g0, 0) + mm(expand, coarse, NN)
    return jnp.concatenate(att, 0), jnp.concatenate(gq, 0), fine, gxk, gxv


def lanes(n, wide):
    return pl.ds(pl.multiple_of(n * wide, wide), wide)


def attention_kernel(bits, q, k, v, k12, v12, c1, z1, z2, z3, y1, y2, y3, ga, *rest, first):
    if first:
        att_o, gq_o, fine_o, near_o, far_o, attt_o = rest
    else:
        far_i, att_o, gq_o, fine_o, near_o, gy1_o, gy2_o, gy3_o, attt_o = rest
        for out, rows in ((gy1_o, slice(0, 32)), (gy2_o, slice(32, 48)), (gy3_o, slice(48, 64))):
            out[:, :D] = far_i[rows, :]
    base = (1 - bits[XH] if first else bits[XH]) * HALF_STEPS
    r = lax.broadcasted_iota(jnp.int32, (T, 192), 0)
    c = lax.broadcasted_iota(jnp.int32, (T, 192), 1)
    half = jnp.where((r >> 1) == c, 0.5, 0.0)
    expand = jnp.where(c < 128, half, jnp.where((r >> 2) == c - 128, 0.25, 0.0)).astype(BF)
    r = lax.broadcasted_iota(jnp.int32, (288, 1), 0)
    bias = jnp.where(r < 64, 0, (r >> 5) - 1).astype(F) * LN2

    def step(i, carry):
        wide, pair = lanes(base + i, W), lanes(base + i, 2 * W)
        qs, ks, vs, gas = q[:, wide], k[:, wide], v[:, wide], ga[:, wide]
        kps, vps = k12[:, wide], v12[:, wide]
        x = jnp.concatenate([p[:, pair] for p in (c1, z1, z2, z3, y1, y2, y3)], 0)
        done = []
        for h in range(HS):
            a = slice(h * HD, h * HD + HD)
            b = slice(W + h * HD, W + h * HD + HD)
            done.append(
                head(qs[:, a], ks[:, a], vs[:, a], kps[:, a], vps[:, a], x[:, a], x[:, b], gas[:, a], bias, expand)
            )
        att = jnp.concatenate([d[0] for d in done], 1)
        att_o[:, lanes(i, W)] = att.astype(BF)
        attt_o[lanes(i, W), :] = jnp.transpose(att).astype(BF)
        gq_o[:, lanes(i, W)] = jnp.concatenate([d[1] for d in done], 1).astype(BF)
        parts = [d[2][:, :HD] for d in done] + [d[2][:, HD:] for d in done]
        fine_o[:, lanes(i, 2 * W)] = jnp.concatenate(parts, 1)
        g = jnp.concatenate([d[3] for d in done] + [d[4] for d in done], 1)
        near_o[:, lanes(i, 2 * W)] = g[:96]
        gb = g[96:].astype(BF)
        if first:
            far_o[:, lanes(i, 2 * W)] = gb
        else:
            to = lanes(i + HALF_STEPS, 2 * W)
            gy1_o[:, to] = gb[:32]
            gy2_o[:, to] = gb[32:48]
            gy3_o[:, to] = gb[48:]
        return carry

    lax.fori_loop(0, HALF_STEPS, step, 0, unroll=UNROLL)


def attention(bits, q, k, v, k12, v12, pieces, ga, *far):
    first = not far
    outs = [((T, D // 2), BF), ((T, D // 2), BF), ((T, D), F), ((96, D), F)]
    outs += [((64, D), BF)] if first else [((32, PAIR), BF), ((16, PAIR), BF), ((16, PAIR), BF)]
    outs += [((D // 2, T), BF)]
    return placed(
        lambda *refs: attention_kernel(*refs, first=first), outs, "attention", 7, 32, bits, q, k, v, k12, v12, *pieces, ga, *far
    )


def placed(kernel, outs, name, us, mib, bits, *operands):
    vmem = pl.BlockSpec(memory_space=pltpu.VMEM)
    return pl.pallas_call(
        lambda *refs: kernel(bits, *refs),
        in_specs=[vmem] * len(operands),
        out_specs=[vmem] * len(outs),
        out_shape=shapes(*outs),
        cost_estimate=cost(us),
        compiler_params=params(mib),
        name=name,
    )(*operands)


def back_row_kernel(near_a, near_b, y1, y2, y3, s1, s2, s3, own):
    g6 = y1[...].astype(F) + spread(y2[...].astype(F) + y3[...].astype(F), 1)
    for i, near in enumerate((near_a, near_b)):
        c = slice(i * D, i * D + D)
        s1[:, c] = (near[32:64, :] + spread(g6[8:16, c], 2)).astype(BF)
        s2[:, c] = (near[64:80, :] + spread(g6[16:24, c], 1)).astype(BF)
        s3[:, c] = (near[80:, :] + spread(g6[24:, c], 1)).astype(BF)
    own[...] = spread(g6[:8], 2)


def back_chip_kernel(near_a, near_b, own, z1, z2, z3, send, keep):
    g4 = own[...] + z1[...].astype(F) + spread(z2[...].astype(F) + z3[...].astype(F), 1)
    for i, near in enumerate((near_a, near_b)):
        c = slice(i * D, i * D + D)
        send[:, c] = (near[:32, :] + spread(g4[16:, c], 1)).astype(BF)
    keep[...] = spread(g4[:16], 1)


def finish_kernel(bits, fine_a, fine_b, keep, c1, gk, gv):
    g3 = spread(keep[...] + c1[...].astype(F), 3)
    for half, (fine, side) in enumerate(((fine_a, 1 - bits[XH]), (fine_b, bits[XH]))):
        for step in range(HALF_STEPS):
            for i, out in enumerate((gk, gv)):
                n = 2 * step + i
                total = fine[:, n * W : n * W + W] + g3[:, half * D + n * W : half * D + n * W + W]
                out[:, lanes(side * HALF_STEPS + step, W)] = total.astype(BF)


def split_kernel(bits, go, go_m, go_o):
    mine = bits[CORE]
    half = D // 2
    go_m[...] = go[:, pl.ds(pl.multiple_of(mine * half, half), half)]
    go_o[...] = go[:, pl.ds(pl.multiple_of((1 - mine) * half, half), half)]


def split(bits, go):
    vmem = pl.BlockSpec(memory_space=pltpu.VMEM)
    return pl.pallas_call(
        lambda *refs: split_kernel(bits, *refs),
        in_specs=[vmem],
        out_specs=[vmem] * 2,
        out_shape=shapes(*[((T, D // 2), BF)] * 2),
        cost_estimate=cost(0.3),
        compiler_params=params(10),
        name="split",
    )(go)


def grad_attended_kernel(go, w, ga):
    for c in range(0, D, 256):
        ga[:, c : c + 256] = mm(go[...], w[c : c + 256, :], NT).astype(BF)


def mixed_kernel(bits, att_a, att_b, w, mixed):
    half = D // 2
    a, b = lanes(1 - bits[XH], half), lanes(bits[XH], half)
    for c in range(0, D, 256):
        cols = slice(c, c + 256)
        mixed[:, cols] = (mm(att_a[...], w[a, cols], NN) + mm(att_b[...], w[b, cols], NN)).astype(BF)


def join_kernel(bits, gq_a, gq_b, gq):
    half = D // 2
    gq[:, lanes(1 - bits[XH], half)] = gq_a[...]
    gq[:, lanes(bits[XH], half)] = gq_b[...]


def small(kernel, outs, name, us=0.4):
    return pl.pallas_call(kernel, out_shape=shapes(*outs), cost_estimate=cost(us),
        compiler_params=params(12), name=name)


def halves(which, outer, half):
    for o in range(outer):
        first = pl.multiple_of((2 * o + which) * half, 16 if half % 16 == 0 else 8)
        yield slice(o * half, o * half + half), pl.ds(first, half)


def weight_kernel(bits, *refs, color, bit, outer, half):
    atts, gos, (send, keep, whole) = refs[:4], refs[4:8], refs[8:]
    c = slice(color * PART, color * PART + PART)
    for rows in range(0, D // 2, 384):
        r = slice(rows, rows + 384)
        whole[r, :] = sum(mm(a[r, :], g[:, c], NN) for a, g in zip(atts, gos, strict=True)).astype(BF)
    away = 1 - bits[bit]
    for out, which in ((send, away), (keep, 1 - away)):
        for to, rows in halves(which, outer, half):
            out[to, :] = whole[rows, :]


def weight(bits, atts, gos, color, bit, outer, half):
    vmem = pl.BlockSpec(memory_space=pltpu.VMEM)
    return pl.pallas_call(
        lambda *refs: weight_kernel(bits, *refs, color=color, bit=bit, outer=outer, half=half),
        in_specs=[vmem] * (2 * len(atts)),
        out_specs=[vmem, vmem],
        out_shape=shapes(((D // 4, PART), BF), ((D // 4, PART), BF)),
        scratch_shapes=[pltpu.VMEM((D // 2, PART), BF)],
        cost_estimate=cost(1.5),
        compiler_params=params(10),
        name="weight_part",
    )(*atts, *gos)


def merge_kernel(bits, *refs, bit, outer, half):
    away = 1 - bits[bit]
    n = (len(refs) - 2) // 2
    for out, which in ((refs[-2], away), (refs[-1], 1 - away)):
        for to, rows in halves(which, outer, half):
            for i in range(n):
                a, b = refs[2 * i], refs[2 * i + 1]
                w = a.shape[1]
                s = a[rows, :].astype(F) + b[rows, :].astype(F)
                out[to, i * w : i * w + w] = s.astype(out.dtype)


def merge(bits, pairs, bit, outer, half, dtype=BF):
    operands = [x for pair in pairs for x in pair]
    wide = sum(pair[0].shape[1] for pair in pairs)
    vmem = pl.BlockSpec(memory_space=pltpu.VMEM)
    return pl.pallas_call(
        lambda *refs: merge_kernel(bits, *refs, bit=bit, outer=outer, half=half),
        in_specs=[vmem] * len(operands),
        out_specs=[vmem, vmem],
        out_shape=shapes(*[((outer * half, wide), dtype)] * 2),
        cost_estimate=cost(0.6),
        compiler_params=params(10),
        name="merge",
    )(*operands)


def last_merge_kernel(bits, kept, got, *outs):
    y, z = bits[YL], bits[ZL]
    total = kept[...].astype(F) + got[...].astype(F)
    quarters = [total[24 * i : 24 * i + 24] for i in range(4)]
    for out, dy, dz in zip(outs, (1, 0, 1, 0), (0, 1, 1, 0), strict=True):
        low = [jnp.where((z ^ dz) == 0, quarters[2 * i], quarters[2 * i + 1]) for i in range(2)]
        out[...] = jnp.where((y ^ dy) == 0, low[0], low[1])


def last_merge(bits, *operands):
    vmem = pl.BlockSpec(memory_space=pltpu.VMEM)
    return pl.pallas_call(
        lambda *refs: last_merge_kernel(bits, *refs),
        in_specs=[vmem] * 2,
        out_specs=[vmem] * 4,
        out_shape=shapes(*[((24, D // 2), F)] * 4),
        cost_estimate=cost(0.6),
        compiler_params=params(10),
        name="last_merge",
    )(*operands)


def tail_kernel(bits, kept, r1, r2, r3, mine, send):
    total = (kept[...] + r1[...]) + (r2[...] + r3[...])
    first = bits[CORE] == 0
    mine[...] = jnp.where(first, total[:12], total[12:])
    send[...] = jnp.where(first, total[12:], total[:12])


def after(x, *others):
    return lax.optimization_barrier((x, *others))[0]


def across(x, flip):
    return lax.ppermute(x, "seq", [(i, i ^ flip) for i in range(32)])


def across_x(x, flip):
    return lax.ppermute(x, "dp", [(i, i ^ flip) for i in range(4)])


def local(query, key, value, w_out, grad_out):
    q, k, v, go = query[0], key[0], value[0], grad_out[0]
    place = lax.axis_index("seq")
    core = place & 1
    bits = Bits()
    k12, k3 = small(key_means_kernel, [((192, D), BF), ((32, D), BF)], "key_means")(k)
    v12, l3 = small(value_means_kernel, [((192, D), BF), ((32, PAIR), BF)], "value_means")(v, k3)
    c1 = across(l3, 1)
    l4, l5 = small(chip_kernel, [((32, PAIR), BF), ((16, PAIR), BF)], "chip")(l3, c1)
    z1, z3, z2 = across(l4, 2), across(l5, 6), across(l5, 4)
    go_m, go_s = split(bits, after(go, l3))
    go_o = across(go_s, 1)
    l5 = after(l5, go_o)
    ga = small(grad_attended_kernel, [((T, D), BF)], "grad_attended", 2.0)(after(go, z1), w_out)[0]
    l6, l7 = small(row_kernel, [((32, PAIR), BF), ((16, PAIR), BF)], "row")(l5, z1, z2, z3)
    gox_m, gox_o = across_x(go_m, 3), across_x(go_o, 3)
    y1, y3, y2 = across(l6, 8), across(l7, 24), across(l7, 16)
    pieces = (c1, z1, z2, z3, y1, y2, y3)
    att_a, gq_a, fine_a, near_a, far, sent = attention(bits, after(q, gox_m, gox_o), k, v, k12, v12, pieces, ga)
    att_x = across_x(sent, 3)
    att_b, gq_b, fine_b, near_b, gy1, gy2, gy3, att_m = attention(
        bits, after(q, sent), k, v, k12, v12, pieces, ga, far
    )
    att_o, att_xo = across(att_m, 1), across(att_x, 1)
    y1, y3, y2 = across(gy1, 8), across(gy3, 24), across(gy2, 16)
    atts = (att_m, att_o, att_x, att_xo)
    gos = (go_m, go_o, gox_m, gox_o)
    b_s, b_k = weight(bits, (att_m, *atts[1:]), gos, 1, ZH, 8, 48)
    b_r = across(b_s, 6)
    a_s, a_k = weight(bits, (after(att_m, b_k), *atts[1:]), gos, 0, XL, 1, 384)
    a_r = across_x(a_s, 1)
    mixed = placed(mixed_kernel, [((T, D), BF)], "mixed", 2.3, 12, bits, after(att_a, a_k), att_b, w_out)[0]
    b_s, b_k = merge(bits, [(after(b_k, mixed), b_r)], XL, 1, 192)
    b_r = across_x(b_s, 1)
    a_s, a_k = merge(bits, [(after(a_k, b_k), a_r)], ZH, 4, 48)
    a_r = across(a_s, 6)
    s1, s2, s3, own = small(
        back_row_kernel, [((32, PAIR), BF), ((16, PAIR), BF), ((16, PAIR), BF), ((32, PAIR), F)], "back_row"
    )(near_a, after(near_b, a_k), y1, y2, y3)
    z1, z3, z2 = across(s1, 2), across(s3, 6), across(s2, 4)
    s, kept = merge(bits, [(after(a_k, own), a_r), (b_k, b_r)], YH, 1, 96)
    s_r = across(s, 24)
    gq = placed(join_kernel, [((T, D), BF)], "join", 0.7, 8, bits, after(gq_a, kept), gq_b)[0]
    send, keep = small(back_chip_kernel, [((32, PAIR), BF), ((32, PAIR), F)], "back_chip")(
        near_a, after(near_b, gq), own, z1, z2, z3
    )
    c1 = across(send, 1)
    s1, s2, s3, kept = last_merge(bits, after(kept, keep), s_r)
    r1, r2, r3 = across(s1, 8), across(s2, 2), across(s3, 10)
    gk, gv = placed(
        finish_kernel, [((T, D), BF)] * 2, "finish", 1.7, 12, bits, after(fine_a, kept), fine_b, keep, c1
    )
    mine, theirs = placed(tail_kernel, [((12, D // 2), F)] * 2, "tail", 0.4, 4, bits, after(kept, gk), r1, r2, r3)
    theirs = across(theirs, 1)
    first = core == 0
    total = jnp.concatenate([jnp.where(first, mine, theirs), jnp.where(first, theirs, mine)], 1)
    gw = total * (1.0 / math.sqrt(4 * 32 * T))
    return mixed[None], gq[None], gk[None], gv[None], gw


def solution(mesh):
    rows = P("dp", "seq", None)
    return jax.shard_map(
        local,
        mesh=mesh,
        in_specs=(rows, rows, rows, P(), rows),
        out_specs=(rows, rows, rows, rows, P(("dp", "seq"), None)),
        check_vma=False,
    )
```

```python
import math

import jax
import jax.numpy as jnp
from jax import lax
from jax.experimental import pallas as pl
from jax.experimental.pallas import tpu as pltpu
from jax.sharding import PartitionSpec as P

H = 12
HD = 128
D = 1536
T = 256
HS = 2
W = HS * HD
STEPS = H // HS
HALF_STEPS = STEPS // 2
UNROLL = True
BF = jnp.bfloat16
F = jnp.float32
NT = (((1,), (1,)), ((), ()))
TN = (((0,), (0,)), ((), ()))
NN = (((1,), (0,)), ((), ()))
LN2 = math.log(2.0)
SCALE = HD**-0.5
PART = D // 4
PAIR = 2 * D


XH, XL, YH, YL, ZH, ZL, CORE = range(7)


class Bits:
    def __getitem__(self, n):
        if n in (XH, XL):
            return lax.axis_index("dp") >> (1 - n) & 1
        return lax.axis_index("seq") >> (CORE - n) & 1


def mm(a, b, dims):
    return lax.dot_general(a, b, dims, preferred_element_type=F)


def params(mib):
    return pltpu.CompilerParams(vmem_limit_bytes=mib * 2**20)


def cost(us):
    return pl.CostEstimate(flops=0, bytes_accessed=int(us * 3.7e6), transcendentals=0)


def shapes(*items):
    return [jax.ShapeDtypeStruct(s, t) for s, t in items]


def fold_matrix(n):
    r = lax.broadcasted_iota(jnp.int32, (n, 2 * n), 0)
    c = lax.broadcasted_iota(jnp.int32, (n, 2 * n), 1)
    return jnp.where((c >> 1) == r, 0.5, 0.0).astype(BF)


def fold(x):
    return mm(fold_matrix(x.shape[0] // 2), x, NN).astype(BF)


def spread(x, bits):
    n = x.shape[0]
    r = lax.broadcasted_iota(jnp.int32, (n << bits, n), 0)
    c = lax.broadcasted_iota(jnp.int32, (n << bits, n), 1)
    return mm(jnp.where((r >> bits) == c, 0.5**bits, 0.0).astype(BF), x.astype(BF), NN)


def means_of(x):
    r = lax.broadcasted_iota(jnp.int32, (224, T), 0)
    c = lax.broadcasted_iota(jnp.int32, (224, T), 1)
    low = jnp.where(r < 192, jnp.where((c >> 2) == r - 128, 0.25, 0.0), jnp.where((c >> 3) == r - 192, 0.125, 0.0))
    means = jnp.where(r < 128, jnp.where((c >> 1) == r, 0.5, 0.0), low).astype(BF)
    return [mm(means, x[:, n * W : n * W + W], NN).astype(BF) for n in range(STEPS)]


def key_means_kernel(k, l12, l3):
    for n, x in enumerate(means_of(k)):
        l12[:, n * W : n * W + W] = x[:192]
        l3[:, n * W : n * W + W] = x[192:]


def value_means_kernel(v, l3_k, l12, l3):
    for n, x in enumerate(means_of(v)):
        l12[:, n * W : n * W + W] = x[:192]
        l3[:, 2 * n * W : (2 * n + 1) * W] = l3_k[:, n * W : n * W + W]
        l3[:, (2 * n + 1) * W : (2 * n + 2) * W] = x[192:]


def chip_kernel(mine, other, l4, l5):
    x = fold(jnp.concatenate([mine[...], other[...]], 0))
    l4[...] = x
    l5[...] = fold(x)


def row_kernel(l5, z1, z2, z3, l6, l7):
    x = fold(jnp.concatenate([l5[...], fold(z1[...]), z2[...], z3[...]], 0))
    l6[...] = x
    l7[...] = fold(x)


def head(q, k0, v0, k12, v12, xk, xv, ga, bias, expand):
    s_all = mm(jnp.concatenate([k0, k12, xk], 0), q, NT)
    g_all = mm(jnp.concatenate([v0, v12, xv], 0), ga, NT)
    low = lax.broadcasted_iota(jnp.int32, (1, 128), 1) < 64
    low64 = jnp.broadcast_to(low, (64, 128))
    low32 = low64[:32]

    def pick(full, j):
        c = full[:, 128 * j : 128 * j + 128]
        a = jnp.where(low, c[128 * j : 128 * j + 64], c[128 * j + 64 : 128 * j + 128])
        b = jnp.where(low, c[288 + 64 * j : 320 + 64 * j], c[256 + 64 * j : 288 + 64 * j])
        d = c[416 - 32 * j : 448 - 32 * j]
        return jnp.concatenate([a, b, d, c[448:608]], 0)

    def widen(x):
        a, b = x[:64], x[64:96]
        za, zb = jnp.zeros_like(a), jnp.zeros_like(b)
        return jnp.concatenate(
            [
                jnp.where(low64, a, za),
                jnp.where(low64, za, a),
                jnp.where(low32, zb, b),
                jnp.where(low32, b, zb),
                x[96:],
            ],
            0,
        )

    att, gq, g0, g1, g2, px, sx = [], [], [], [], [None, None], [], []
    for j in range(2):
        s = pick(s_all, j) * SCALE + bias
        e = jnp.exp(s - jnp.max(s, axis=0, keepdims=True))
        p = e * (1.0 / jnp.sum(e, axis=0, keepdims=True))
        pb = p.astype(BF)
        gp = pick(g_all, j)
        delta = jnp.sum(pb.astype(F) * gp, axis=0, keepdims=True)
        gs = (p * (gp - delta) * SCALE).astype(BF)
        pw, sw = widen(pb), widen(gs)
        rows, o = slice(128 * j, 128 * j + 128), 1 - j
        near = slice(64 * j, 64 * j + 64)
        far = slice(128 + 32 * o, 160 + 32 * o)
        kh = jnp.concatenate([k0[rows], k12[near], k12[far], xk], 0)
        vh = jnp.concatenate([v0[rows], v12[near], v12[far], xv], 0)
        att.append(mm(pw, vh, TN))
        gq.append(mm(sw, kh, TN))
        both = jnp.concatenate([mm(sw[:224], q[rows], NN), mm(pw[:224], ga[rows], NN)], 1)
        g0.append(both[:128])
        g1.append(both[128:192])
        g2[o] = both[192:224]
        px.append(pw[224:])
        sx.append(sw[224:])
    gxk = mm(jnp.concatenate(sx, 1), q, NN)
    gxv = mm(jnp.concatenate(px, 1), ga, NN)
    coarse = jnp.concatenate(g1 + g2, 0).astype(BF)
    fine = jnp.concatenate(g0, 0) + mm(expand, coarse, NN)
    return jnp.concatenate(att, 0), jnp.concatenate(gq, 0), fine, gxk, gxv


def lanes(n, wide):
    return pl.ds(pl.multiple_of(n * wide, wide), wide)


def attention_kernel(bits, q, k, v, k12, v12, c1, z1, z2, z3, y1, y2, y3, ga, *rest, first):
    if first:
        att_o, gq_o, fine_o, near_o, far_o, attt_o = rest
    else:
        far_i, att_o, gq_o, fine_o, near_o, gy1_o, gy2_o, gy3_o, attt_o = rest
        for out, rows in ((gy1_o, slice(0, 32)), (gy2_o, slice(32, 48)), (gy3_o, slice(48, 64))):
            out[:, :D] = far_i[rows, :]
    base = (1 - bits[XH] if first else bits[XH]) * HALF_STEPS
    r = lax.broadcasted_iota(jnp.int32, (T, 192), 0)
    c = lax.broadcasted_iota(jnp.int32, (T, 192), 1)
    half = jnp.where((r >> 1) == c, 0.5, 0.0)
    expand = jnp.where(c < 128, half, jnp.where((r >> 2) == c - 128, 0.25, 0.0)).astype(BF)
    r = lax.broadcasted_iota(jnp.int32, (288, 1), 0)
    bias = jnp.where(r < 64, 0, (r >> 5) - 1).astype(F) * LN2

    def step(i, carry):
        wide, pair = lanes(base + i, W), lanes(base + i, 2 * W)
        qs, ks, vs, gas = q[:, wide], k[:, wide], v[:, wide], ga[:, wide]
        kps, vps = k12[:, wide], v12[:, wide]
        x = jnp.concatenate([p[:, pair] for p in (c1, z1, z2, z3, y1, y2, y3)], 0)
        done = []
        for h in range(HS):
            a = slice(h * HD, h * HD + HD)
            b = slice(W + h * HD, W + h * HD + HD)
            done.append(
                head(qs[:, a], ks[:, a], vs[:, a], kps[:, a], vps[:, a], x[:, a], x[:, b], gas[:, a], bias, expand)
            )
        att = jnp.concatenate([d[0] for d in done], 1)
        att_o[:, lanes(i, W)] = att.astype(BF)
        attt_o[lanes(i, W), :] = jnp.transpose(att).astype(BF)
        gq_o[:, lanes(i, W)] = jnp.concatenate([d[1] for d in done], 1).astype(BF)
        parts = [d[2][:, :HD] for d in done] + [d[2][:, HD:] for d in done]
        fine_o[:, lanes(i, 2 * W)] = jnp.concatenate(parts, 1)
        g = jnp.concatenate([d[3] for d in done] + [d[4] for d in done], 1)
        near_o[:, lanes(i, 2 * W)] = g[:96]
        gb = g[96:].astype(BF)
        if first:
            far_o[:, lanes(i, 2 * W)] = gb
        else:
            to = lanes(i + HALF_STEPS, 2 * W)
            gy1_o[:, to] = gb[:32]
            gy2_o[:, to] = gb[32:48]
            gy3_o[:, to] = gb[48:]
        return carry

    lax.fori_loop(0, HALF_STEPS, step, 0, unroll=UNROLL)


def attention(bits, q, k, v, k12, v12, pieces, ga, *far):
    first = not far
    outs = [((T, D // 2), BF), ((T, D // 2), BF), ((T, D), F), ((96, D), F)]
    outs += [((64, D), BF)] if first else [((32, PAIR), BF), ((16, PAIR), BF), ((16, PAIR), BF)]
    outs += [((D // 2, T), BF)]
    return placed(
        lambda *refs: attention_kernel(*refs, first=first), outs, "attention", 7, 32, bits, q, k, v, k12, v12, *pieces, ga, *far
    )


def placed(kernel, outs, name, us, mib, bits, *operands):
    vmem = pl.BlockSpec(memory_space=pltpu.VMEM)
    return pl.pallas_call(
        lambda *refs: kernel(bits, *refs),
        in_specs=[vmem] * len(operands),
        out_specs=[vmem] * len(outs),
        out_shape=shapes(*outs),
        cost_estimate=cost(us),
        compiler_params=params(mib),
        name=name,
    )(*operands)


def back_row_kernel(near_a, near_b, y1, y2, y3, s1, s2, s3, own):
    g6 = y1[...].astype(F) + spread(y2[...].astype(F) + y3[...].astype(F), 1)
    for i, near in enumerate((near_a, near_b)):
        c = slice(i * D, i * D + D)
        s1[:, c] = (near[32:64, :] + spread(g6[8:16, c], 2)).astype(BF)
        s2[:, c] = (near[64:80, :] + spread(g6[16:24, c], 1)).astype(BF)
        s3[:, c] = (near[80:, :] + spread(g6[24:, c], 1)).astype(BF)
    own[...] = spread(g6[:8], 2)


def back_chip_kernel(near_a, near_b, own, z1, z2, z3, send, keep):
    g4 = own[...] + z1[...].astype(F) + spread(z2[...].astype(F) + z3[...].astype(F), 1)
    for i, near in enumerate((near_a, near_b)):
        c = slice(i * D, i * D + D)
        send[:, c] = (near[:32, :] + spread(g4[16:, c], 1)).astype(BF)
    keep[...] = spread(g4[:16], 1)


def finish_kernel(bits, fine_a, fine_b, keep, c1, gk, gv):
    g3 = spread(keep[...] + c1[...].astype(F), 3)
    for half, (fine, side) in enumerate(((fine_a, 1 - bits[XH]), (fine_b, bits[XH]))):
        for step in range(HALF_STEPS):
            for i, out in enumerate((gk, gv)):
                n = 2 * step + i
                total = fine[:, n * W : n * W + W] + g3[:, half * D + n * W : half * D + n * W + W]
                out[:, lanes(side * HALF_STEPS + step, W)] = total.astype(BF)


def split_kernel(bits, go, go_m, go_o):
    mine = bits[CORE]
    half = D // 2
    go_m[...] = go[:, pl.ds(pl.multiple_of(mine * half, half), half)]
    go_o[...] = go[:, pl.ds(pl.multiple_of((1 - mine) * half, half), half)]


def split(bits, go):
    vmem = pl.BlockSpec(memory_space=pltpu.VMEM)
    return pl.pallas_call(
        lambda *refs: split_kernel(bits, *refs),
        in_specs=[vmem],
        out_specs=[vmem] * 2,
        out_shape=shapes(*[((T, D // 2), BF)] * 2),
        cost_estimate=cost(0.3),
        compiler_params=params(10),
        name="split",
    )(go)


def grad_attended_kernel(go, w, ga):
    for c in range(0, D, 256):
        ga[:, c : c + 256] = mm(go[...], w[c : c + 256, :], NT).astype(BF)


def mixed_kernel(bits, att_a, att_b, w, mixed):
    half = D // 2
    a, b = lanes(1 - bits[XH], half), lanes(bits[XH], half)
    for c in range(0, D, 256):
        cols = slice(c, c + 256)
        mixed[:, cols] = (mm(att_a[...], w[a, cols], NN) + mm(att_b[...], w[b, cols], NN)).astype(BF)


def join_kernel(bits, gq_a, gq_b, gq):
    half = D // 2
    gq[:, lanes(1 - bits[XH], half)] = gq_a[...]
    gq[:, lanes(bits[XH], half)] = gq_b[...]


def small(kernel, outs, name, us=0.4):
    return pl.pallas_call(kernel, out_shape=shapes(*outs), cost_estimate=cost(us),
        compiler_params=params(12), name=name)


def halves(which, outer, half):
    for o in range(outer):
        first = pl.multiple_of((2 * o + which) * half, 16 if half % 16 == 0 else 8)
        yield slice(o * half, o * half + half), pl.ds(first, half)


def weight_kernel(bits, *refs, color, bit, outer, half):
    atts, gos, (send, keep, whole) = refs[:4], refs[4:8], refs[8:]
    c = slice(color * PART, color * PART + PART)
    for rows in range(0, D // 2, 384):
        r = slice(rows, rows + 384)
        whole[r, :] = sum(mm(a[r, :], g[:, c], NN) for a, g in zip(atts, gos, strict=True)).astype(BF)
    away = 1 - bits[bit]
    for out, which in ((send, away), (keep, 1 - away)):
        for to, rows in halves(which, outer, half):
            out[to, :] = whole[rows, :]


def weight(bits, atts, gos, color, bit, outer, half):
    vmem = pl.BlockSpec(memory_space=pltpu.VMEM)
    return pl.pallas_call(
        lambda *refs: weight_kernel(bits, *refs, color=color, bit=bit, outer=outer, half=half),
        in_specs=[vmem] * (2 * len(atts)),
        out_specs=[vmem, vmem],
        out_shape=shapes(((D // 4, PART), BF), ((D // 4, PART), BF)),
        scratch_shapes=[pltpu.VMEM((D // 2, PART), BF)],
        cost_estimate=cost(1.5),
        compiler_params=params(10),
        name="weight_part",
    )(*atts, *gos)


def merge_kernel(bits, *refs, bit, outer, half):
    away = 1 - bits[bit]
    n = (len(refs) - 2) // 2
    for out, which in ((refs[-2], away), (refs[-1], 1 - away)):
        for to, rows in halves(which, outer, half):
            for i in range(n):
                a, b = refs[2 * i], refs[2 * i + 1]
                w = a.shape[1]
                s = a[rows, :].astype(F) + b[rows, :].astype(F)
                out[to, i * w : i * w + w] = s.astype(out.dtype)


def merge(bits, pairs, bit, outer, half, dtype=BF):
    operands = [x for pair in pairs for x in pair]
    wide = sum(pair[0].shape[1] for pair in pairs)
    vmem = pl.BlockSpec(memory_space=pltpu.VMEM)
    return pl.pallas_call(
        lambda *refs: merge_kernel(bits, *refs, bit=bit, outer=outer, half=half),
        in_specs=[vmem] * len(operands),
        out_specs=[vmem, vmem],
        out_shape=shapes(*[((outer * half, wide), dtype)] * 2),
        cost_estimate=cost(0.6),
        compiler_params=params(10),
        name="merge",
    )(*operands)


def last_merge_kernel(bits, kept, got, *outs):
    y, z = bits[YL], bits[ZL]
    total = kept[...].astype(F) + got[...].astype(F)
    quarters = [total[24 * i : 24 * i + 24] for i in range(4)]
    for out, dy, dz in zip(outs, (1, 0, 1, 0), (0, 1, 1, 0), strict=True):
        low = [jnp.where((z ^ dz) == 0, quarters[2 * i], quarters[2 * i + 1]) for i in range(2)]
        out[...] = jnp.where((y ^ dy) == 0, low[0], low[1])


def last_merge(bits, *operands):
    vmem = pl.BlockSpec(memory_space=pltpu.VMEM)
    return pl.pallas_call(
        lambda *refs: last_merge_kernel(bits, *refs),
        in_specs=[vmem] * 2,
        out_specs=[vmem] * 4,
        out_shape=shapes(*[((24, D // 2), F)] * 4),
        cost_estimate=cost(0.6),
        compiler_params=params(10),
        name="last_merge",
    )(*operands)


def tail_kernel(bits, kept, r1, r2, r3, mine, send):
    total = (kept[...] + r1[...]) + (r2[...] + r3[...])
    first = bits[CORE] == 0
    mine[...] = jnp.where(first, total[:12], total[12:])
    send[...] = jnp.where(first, total[12:], total[:12])


def after(x, *others):
    return lax.optimization_barrier((x, *others))[0]


def across(x, flip):
    return lax.ppermute(x, "seq", [(i, i ^ flip) for i in range(32)])


def across_x(x, flip):
    return lax.ppermute(x, "dp", [(i, i ^ flip) for i in range(4)])


def local(query, key, value, w_out, grad_out):
    q, k, v, go = query[0], key[0], value[0], grad_out[0]
    place = lax.axis_index("seq")
    core = place & 1
    bits = Bits()
    k12, k3 = small(key_means_kernel, [((192, D), BF), ((32, D), BF)], "key_means")(k)
    v12, l3 = small(value_means_kernel, [((192, D), BF), ((32, PAIR), BF)], "value_means")(v, k3)
    c1 = across(l3, 1)
    l4, l5 = small(chip_kernel, [((32, PAIR), BF), ((16, PAIR), BF)], "chip")(l3, c1)
    z1, z3, z2 = across(l4, 2), across(l5, 6), across(l5, 4)
    go_m, go_s = split(bits, after(go, l3))
    go_o = across(go_s, 1)
    l5 = after(l5, go_o)
    ga = small(grad_attended_kernel, [((T, D), BF)], "grad_attended", 2.0)(after(go, z1), w_out)[0]
    l6, l7 = small(row_kernel, [((32, PAIR), BF), ((16, PAIR), BF)], "row")(l5, z1, z2, z3)
    gox_m, gox_o = across_x(go_m, 3), across_x(go_o, 3)
    y1, y3, y2 = across(l6, 8), across(l7, 24), across(l7, 16)
    pieces = (c1, z1, z2, z3, y1, y2, y3)
    att_a, gq_a, fine_a, near_a, far, sent = attention(bits, after(q, gox_m, gox_o), k, v, k12, v12, pieces, ga)
    att_x = across_x(sent, 3)
    att_b, gq_b, fine_b, near_b, gy1, gy2, gy3, att_m = attention(
        bits, after(q, sent), k, v, k12, v12, pieces, ga, far
    )
    att_o, att_xo = across(att_m, 1), across(att_x, 1)
    y1, y3, y2 = across(gy1, 8), across(gy3, 24), across(gy2, 16)
    atts = (att_m, att_o, att_x, att_xo)
    gos = (go_m, go_o, gox_m, gox_o)
    b_s, b_k = weight(bits, (att_m, *atts[1:]), gos, 1, ZH, 8, 48)
    b_r = across(b_s, 6)
    a_s, a_k = weight(bits, (after(att_m, b_k), *atts[1:]), gos, 0, XL, 1, 384)
    a_r = across_x(a_s, 1)
    mixed = placed(mixed_kernel, [((T, D), BF)], "mixed", 2.3, 12, bits, after(att_a, a_k), att_b, w_out)[0]
    b_s, b_k = merge(bits, [(after(b_k, mixed), b_r)], XL, 1, 192)
    b_r = across_x(b_s, 1)
    a_s, a_k = merge(bits, [(after(a_k, b_k), a_r)], ZH, 4, 48)
    a_r = across(a_s, 6)
    s1, s2, s3, own = small(
        back_row_kernel, [((32, PAIR), BF), ((16, PAIR), BF), ((16, PAIR), BF), ((32, PAIR), F)], "back_row"
    )(near_a, after(near_b, a_k), y1, y2, y3)
    z1, z3, z2 = across(s1, 2), across(s3, 6), across(s2, 4)
    s, kept = merge(bits, [(after(a_k, own), a_r), (b_k, b_r)], YH, 1, 96)
    s_r = across(s, 24)
    send, keep = small(back_chip_kernel, [((32, PAIR), BF), ((32, PAIR), F)], "back_chip")(
        near_a, after(near_b, kept), own, z1, z2, z3
    )
    c1 = across(send, 1)
    gq = placed(join_kernel, [((T, D), BF)], "join", 0.7, 8, bits, after(gq_a, keep), gq_b)[0]
    s1, s2, s3, kept = last_merge(bits, after(kept, gq), s_r)
    r1, r2, r3 = across(s1, 8), across(s2, 2), across(s3, 10)
    gk, gv = placed(
        finish_kernel, [((T, D), BF)] * 2, "finish", 1.7, 12, bits, after(fine_a, kept), fine_b, keep, c1
    )
    mine, theirs = placed(tail_kernel, [((12, D // 2), F)] * 2, "tail", 0.4, 4, bits, after(kept, gk), r1, r2, r3)
    theirs = across(theirs, 1)
    first = core == 0
    total = jnp.concatenate([jnp.where(first, mine, theirs), jnp.where(first, theirs, mine)], 1)
    gw = total * (1.0 / math.sqrt(4 * 32 * T))
    return mixed[None], gq[None], gk[None], gv[None], gw


def solution(mesh):
    rows = P("dp", "seq", None)
    return jax.shard_map(
        local,
        mesh=mesh,
        in_specs=(rows, rows, rows, P(), rows),
        out_specs=(rows, rows, rows, rows, P(("dp", "seq"), None)),
        check_vma=False,
    )
```
